256 devices in a mesh: depth: 4 (over y), lat: 64 (over x, z, core).
Axes of the slice: x: 4, y: 4, z: 8, core: 2. Of those that a mesh axis runs over, the one named last changes fastest.
Arguments:
- diag_blocks: float32 [4, 256, 128, 128], P('depth', 'lat'), as said below
- coupling: float32 [4, 256, 8, 128, 128], P('depth', 'lat'), may hold values from -0.2 to 0.2
- offsets: int32 [4, 256, 8], P('depth', 'lat'), may hold values from -8 to 7, as said below
- arrow_blocks: float32 [4, 256, 4, 128, 128], P('depth', 'lat'), may hold values from -0.9 to 0.9
- arrow_index: int32 [4, 256, 4], P('depth', 'lat'), may hold values from 0 to 7, all different within a row
- tip: float32 [1024, 1024], replicated, may hold values from -6 to 6
Outputs:
- factor: float32 [4, 256, 128, 128], P('depth', 'lat')
- handed: float32 [4, 256, 128, 128], P('depth', 'lat')
- schur_tip: float32 [1024, 1024], replicated
The draws below stay inside these ranges and needn't reach their ends.
Inputs may be any that keep to these rules, and one draw needn't show every extreme that they name: The 8 offsets of one block row are different. `arrow_index`: the 4 indices of one block row are different. `diag_blocks`: each block is symmetric positive definite.
All inputs are finite; a program needn't handle non-finite values.
Results may differ from the reference program's by a relative error of at most 0.0003.
Values sent between devices are 32-bit elements; how exact they have to be, the bound alone decides.
A program may use at most 128 MiB of HBM per device.

```python
import jax
import jax.numpy as jnp
from jax import lax

BS = 128
W = 8
REACH = 8
MB = 8
AS = 4
LAYERS = 4
NB = 256
ARROW = 1024


def draw_diag_blocks(key, part):
    key = jax.random.fold_in(key, 11)
    first, second = jax.random.split(key)
    raw = 0.2 * jax.random.truncated_normal(first, -3.0, 3.0, (LAYERS, NB, BS, BS), jnp.float32)
    symmetric = (raw + jnp.swapaxes(raw, 2, 3)) * 0.7071
    levels = jnp.exp(jax.random.uniform(second, (LAYERS, NB, BS), jnp.float32, jnp.log(8.0), jnp.log(16.0)))
    identity = jnp.eye(BS, dtype=jnp.float32)
    return symmetric + levels[:, :, :, None] * identity[None, None, :, :]


def draw_coupling(key, part):
    key = jax.random.fold_in(key, 37)
    base = jax.random.uniform(key, (LAYERS, NB, W, BS, BS), jnp.float32, -1.0, 1.0)
    values = 0.2 * base
    return values


def draw_offsets(key, part):
    key = jax.random.fold_in(key, 23)
    row_keys = jax.random.split(key, LAYERS * NB)
    orders = jax.vmap(lambda one_key: jax.random.permutation(one_key, 2 * REACH))(row_keys)
    picked = orders[:, :W].astype(jnp.int32) - REACH
    return picked.reshape(LAYERS, NB, W)


def steps_of(own_key, dims, cuts, low, high):
    loudness = 1.0
    for position, blocks in cuts:
        draws = jax.random.uniform(jax.random.fold_in(jax.random.fold_in(own_key, 6), position), (blocks,), jnp.float32, low / len(cuts), high / len(cuts))
        loudness = loudness * jnp.repeat(jnp.exp(draws), dims[position] // blocks).reshape((-1,) + (1,) * (len(dims) - 1 - position))
    return loudness


def choose_distinct(key, rows, count, top, lift):
    order = jax.random.permutation(jax.random.fold_in(key, 1), count)
    favour = order
    for power in range(3):
        favour = favour * favour // count
    favour = favour * lift // count
    tickets = jax.random.randint(jax.random.fold_in(key, 2), (rows, count), 0, 4096) + favour
    fixed_rows = jax.random.permutation(jax.random.fold_in(key, 3), rows)[jnp.arange(count) % rows]
    tickets = jnp.where(jnp.arange(rows)[:, None] == fixed_rows[None, :], 1 << 14, tickets)
    score = tickets * count + jnp.arange(count)
    return lax.top_k(score.astype(jnp.int32), top)[1].astype(jnp.int32)


def bell_draw(key, extent, deviation, reach, shards=(), kind=jnp.bfloat16):
    level = steps_of(key, extent, shards, -0.22, 0.18) if shards else 1.0
    drawn = jax.random.normal(key, extent, jnp.float32) * deviation * level
    return jnp.minimum(jnp.maximum(drawn, -reach), reach).astype(kind)


def setup_inputs(seed: int = 0) -> dict:
    keys = jax.random.split(jax.random.key(seed), 7)
    return {
        "diag_blocks": draw_diag_blocks(jax.random.fold_in(keys[6], 71), 0),
        "coupling": draw_coupling(jax.random.fold_in(keys[6], 71), 0),
        "offsets": draw_offsets(jax.random.fold_in(keys[6], 71), 0),
        "arrow_blocks": bell_draw(keys[3], (LAYERS, NB, AS, BS, BS), 0.15, 0.9, ((0, 4), (1, 64)), jnp.float32),
        "arrow_index": choose_distinct(keys[4], LAYERS * NB, MB, AS, 0).reshape((LAYERS, NB, AS)),
        "tip": bell_draw(keys[5], (ARROW, ARROW), 1.0, 6.0, (), jnp.float32),
    }


HIGH = lax.Precision.HIGHEST

def factor_one(matrix):
    lower_factor = jnp.linalg.cholesky(matrix)
    identity = jnp.eye(matrix.shape[0], dtype=matrix.dtype)
    inverse = jax.scipy.linalg.cho_solve((lower_factor, True), identity)
    return (lower_factor, inverse)

def factorize(blocks):
    return jax.vmap(factor_one)(blocks)

def schur_update(chosen, coupling):
    inner = jnp.einsum('nwbc,nwcd->nwbd', chosen, coupling, precision=HIGH)
    return -jnp.einsum('nwba,nwbd->nad', coupling, inner, precision=HIGH)

def arrow_term(inverse, blocks, index, arrow_count):
    block_size = blocks.shape[-1]
    placing = (index[:, :, None] == jnp.arange(arrow_count, dtype=jnp.int32)[None, None, :]).astype(jnp.float32)
    carried = jnp.einsum('nab,nsbc->nsac', inverse, blocks, precision=HIGH)
    inner = jnp.einsum('nsba,ntbc->nsatc', blocks, carried, precision=HIGH)
    placed = jnp.einsum('ntq,nsatc->nsaqc', placing, inner, precision=HIGH)
    total = jnp.einsum('nsm,nsaqc->maqc', placing, placed, precision=HIGH)
    return total.reshape(arrow_count * block_size, arrow_count * block_size)

def layer_term(item):
    return arrow_term(item[0], item[1], item[2], MB)

def reference(diag_blocks, coupling, offsets, arrow_blocks, arrow_index, tip):
    incoming = jnp.zeros(diag_blocks.shape[1:], jnp.float32)
    lowers = []
    updates = []
    inverses = []
    for layer in range(LAYERS):
        lower_factor, inverse = factorize(diag_blocks[layer] + incoming)
        padded = jnp.pad(inverse, ((REACH, REACH), (0, 0), (0, 0)))
        source = jnp.arange(NB, dtype=jnp.int32)[:, None] + offsets[layer] + REACH
        update = schur_update(padded[source], coupling[layer])
        lowers.append(lower_factor)
        updates.append(update)
        inverses.append(inverse)
        incoming = update
    terms = lax.map(layer_term, (jnp.stack(inverses), arrow_blocks, arrow_index))
    schur_tip = tip - jnp.sum(terms, 0)
    return (jnp.stack(lowers), jnp.stack(updates), schur_tip)
```

```python
import functools

import jax
import jax.numpy as jnp
from jax import lax
from jax.experimental import pallas as pl
from jax.experimental.pallas import tpu as pltpu
from jax.sharding import PartitionSpec as P

BS = 128
PANEL = 32
REACH = 8
MB = 8
F32 = jnp.float32
BF16 = jnp.bfloat16
VMEM = pl.BlockSpec(memory_space=pltpu.VMEM)
SMEM = pl.BlockSpec(memory_space=pltpu.SMEM)
MESH = pl.DeviceIdType.MESH
TILES = [(i, j) for i in range(MB) for j in range(i + 1)]
X, Z = 4, 8


def split2(x):
    high = x.astype(BF16)
    return high, (x - high.astype(F32)).astype(BF16)


def split3(x):
    high = x.astype(BF16)
    rest = x - high.astype(F32)
    middle = rest.astype(BF16)
    return high, middle, (rest - middle.astype(F32)).astype(BF16)


def dot(a, b):
    return jnp.dot(a, b, preferred_element_type=F32)


def dot_t(a, b):
    return lax.dot_general(a, b, (((0,), (0,)), ((), ())), preferred_element_type=F32)


def gram_exact(u, v):
    uh, um, ul = split3(u)
    vh, vm, vl = split3(v)
    return dot_t(
        jnp.concatenate([uh, uh, uh, um, um, ul], 0),
        jnp.concatenate([vh, vm, vl, vh, vm, vh], 0),
    )


def factor_kernel(a_ref, inc_ref, u_ref):
    count = a_ref.shape[0]
    lane = lax.broadcasted_iota(jnp.int32, (8, BS), 1)
    sub = lax.broadcasted_iota(jnp.int32, (8, BS), 0)
    groups = PANEL // 8
    spread = lambda x: jnp.broadcast_to(x, (8, BS))
    first = (lax.axis_index("depth") > 0).astype(F32)
    for m in range(count):
        u_ref[m] = jnp.where(first > 0, a_ref[m] + inc_ref[m], a_ref[m])
    for j0 in range(0, BS, PANEL):
        rows_of = [[u_ref[m, j0 + 8 * v : j0 + 8 * v + 8, :] for v in range(groups)] for m in range(count)]
        for g in range(groups):
            c0 = j0 + 8 * g
            for m in range(count):
                part = rows_of[m]
                cols = [[spread(part[v][:, c0 + k : c0 + k + 1]) for k in range(8)] for v in range(g, groups)]
                keep = (lane < c0) | (lane >= c0 + 8)
                x = jnp.where(keep, part[g], jnp.where(lane == c0 + sub, 1.0, 0.0))
                d = cols[0]
                scales, rows, low = [], [], {}
                for i in range(8):
                    scale = lax.rsqrt(spread(d[i][i : i + 1, :]))
                    li = d[i] * scale
                    for k in range(i + 1, 8):
                        low[k, i] = spread(li[k : k + 1, :])
                        d[k] = d[k] - li * low[k, i]
                    row = spread(x[i : i + 1, :]) * scale
                    scales.append(scale)
                    rows.append(row)
                    x = jnp.where(sub > i, x - li * row, jnp.where(sub == i, row, x))
                for k in range(1, 8):
                    for i in range(k):
                        x = jnp.where((sub == i) & (lane == c0 + k), low[k, i], x)
                part[g] = x
                for v in range(g + 1, groups):
                    d = cols[v - g]
                    x = jnp.where(keep, part[v], 0.0)
                    for i in range(8):
                        mi = d[i] * scales[i]
                        for k in range(i + 1, 8):
                            d[k] = d[k] - mi * low[k, i]
                        x = x - mi * rows[i]
                    part[v] = x
        for m in range(count):
            u = jnp.concatenate(rows_of[m], 0)
            u_ref[m, j0 : j0 + PANEL, :] = u
            end = j0 + PANEL
            if end < BS:
                ln = lax.broadcasted_iota(jnp.int32, u.shape, 1)
                sb = lax.broadcasted_iota(jnp.int32, u.shape, 0)
                full = gram_exact(u, jnp.where((ln < end) & (ln > j0 + sb), 0.0, u))
                rest = u_ref[m, end:, :]
                ln = lax.broadcasted_iota(jnp.int32, rest.shape, 1)
                rest = jnp.where((ln >= j0) & (ln < end), 0.0, rest)
                u_ref[m, end:, :] = rest - full[end:, :]


def factorize(blocks, incoming):
    return pl.pallas_call(
        factor_kernel,
        out_shape=jax.ShapeDtypeStruct(blocks.shape, F32),
        in_specs=[VMEM, VMEM],
        out_specs=VMEM,
    )(blocks, incoming)


def lower_part(u):
    row = lax.broadcasted_iota(jnp.int32, (BS, BS), 0)
    col = lax.broadcasted_iota(jnp.int32, (BS, BS), 1)
    return jnp.where(col <= row, u, 0.0)


def update_kernel(u_ref, c_ref, off_ref, handed_ref, inc_ref, window, wide, stacked, landed, lat_send, lat_recv, dep_send, dep_recv):
    depths, lats = lax.axis_size("depth"), lax.axis_size("lat")
    d, l = lax.axis_index("depth"), lax.axis_index("lat")
    count, width = off_ref.shape
    reach = REACH // count
    steps = [s for s in range(-reach, reach + 1) if s != 0]
    after, before = lax.rem(d + 1, depths), lax.rem(d + depths - 1, depths)

    barrier = pltpu.get_barrier_semaphore()
    for s in steps:
        pl.semaphore_signal(barrier, inc=1, device_id=(d, lax.rem(l + s + lats, lats)), device_id_type=MESH)
    pl.semaphore_signal(barrier, inc=1, device_id=(before, l), device_id_type=MESH)
    for m in range(count):
        window[REACH + m] = lower_part(u_ref[m])
    pl.semaphore_wait(barrier, len(steps) + 1)

    copies = []
    for at, s in enumerate(steps):
        copy = pltpu.make_async_remote_copy(
            src_ref=window.at[pl.ds(REACH, count)],
            dst_ref=window.at[pl.ds(REACH - s * count, count)],
            send_sem=lat_send.at[at],
            recv_sem=lat_recv.at[at],
            device_id=(d, lax.rem(l + s + lats, lats)),
            device_id_type=MESH,
        )
        copy.start()
        copies.append(copy)
    for copy in copies:
        copy.wait()
    for at in range(2 * REACH + count):
        distance = at // count - reach
        inside = (l + distance >= 0) & (l + distance < lats)
        high, low = split2(jnp.where(inside, window[at], 0.0))
        wide[at] = jnp.concatenate([high, low, high], 1)
    sends = []
    for m in range(count):
        for w in range(width):
            ch, cl = split2(c_ref[m, w])
            x = dot(wide[off_ref[m, w] + (m + REACH)], jnp.concatenate([ch, ch, cl], 0))
            xh, xl = split2(x)
            stacked[w * BS : (w + 1) * BS, :] = jnp.concatenate([xh, xl], 1)
        both = dot_t(stacked[:, :BS], stacked[...])
        cross = both[:, BS:]
        handed_ref[m] = -(both[:, :BS] + cross + cross.T)
        copy = pltpu.make_async_remote_copy(
            src_ref=handed_ref.at[m],
            dst_ref=landed.at[m],
            send_sem=dep_send.at[m],
            recv_sem=dep_recv.at[m],
            device_id=(after, l),
            device_id_type=MESH,
        )
        copy.start()
        sends.append(copy)
    for copy in sends:
        copy.wait()
    inc_ref[...] = landed[...]


def exchange(u, coupling, offsets, step):
    count, width = offsets.shape
    shape = jax.ShapeDtypeStruct((count, BS, BS), F32)
    neighbours = 2 * (REACH // count)
    return pl.pallas_call(
        update_kernel,
        out_shape=(shape, shape),
        in_specs=[VMEM, VMEM, SMEM],
        out_specs=(VMEM, VMEM),
        scratch_shapes=[
            pltpu.VMEM((2 * REACH + count, BS, BS), F32),
            pltpu.VMEM((2 * REACH + count, BS, 3 * BS), BF16),
            pltpu.VMEM((width * BS, 2 * BS), BF16),
            pltpu.VMEM((count, BS, BS), F32),
            pltpu.SemaphoreType.DMA((neighbours,)),
            pltpu.SemaphoreType.DMA((neighbours,)),
            pltpu.SemaphoreType.DMA((count,)),
            pltpu.SemaphoreType.DMA((count,)),
        ],
        compiler_params=pltpu.CompilerParams(
            collective_id=step, has_side_effects=True, vmem_limit_bytes=40 * 1024 * 1024
        ),
    )(u, coupling, offsets)


def arrow_kernel(u_ref, b_ref, idx_ref, g_ref, l_ref, left, right):
    count, width = idx_ref.shape
    row = lax.broadcasted_iota(jnp.int32, (BS, BS), 0)
    col = lax.broadcasted_iota(jnp.int32, (BS, BS), 1)
    g_ref[...] = jnp.zeros_like(g_ref)
    for n in range(count):
        u = u_ref[n]
        l_ref[n] = jnp.where(col > row, u, jnp.where(col == row, 1.0 / u, 0.0)).T
        high, low = split2(jnp.where(col <= row, u, 0.0))
        lhs = jnp.concatenate([high, low, high], 1)
        ranks = []
        for s in range(width):
            rank = 0
            for t in range(width):
                if t != s:
                    rank = rank + (idx_ref[n, t] < idx_ref[n, s]).astype(jnp.int32)
            ranks.append(rank)
        for s in range(width):
            bh, bl = split2(b_ref[n, s])
            th, tl = split2(dot(lhs, jnp.concatenate([bh, bh, bl], 0)))
            at = pl.ds(pl.multiple_of(ranks[s] * BS, BS), BS)
            left[:, at] = jnp.concatenate([th, th, tl], 0)
            right[:, at] = jnp.concatenate([th, tl, th], 0)
        sorted_idx = [
            sum(jnp.where(ranks[s] == a, idx_ref[n, s], 0) for s in range(width)) for a in range(width)
        ]
        for a in range(width):
            products = dot_t(left[:, a * BS : (a + 1) * BS], right[:, : (a + 1) * BS])
            for b in range(a + 1):
                i, j = sorted_idx[a], sorted_idx[b]
                g_ref[i * (i + 1) // 2 + j] += products[:, b * BS : (b + 1) * BS]


def arrow_terms(u, blocks, index):
    count, width = index.shape
    return pl.pallas_call(
        arrow_kernel,
        out_shape=(jax.ShapeDtypeStruct((len(TILES), BS, BS), F32), jax.ShapeDtypeStruct(u.shape, F32)),
        in_specs=[VMEM, VMEM, SMEM],
        out_specs=(VMEM, VMEM),
        scratch_shapes=[pltpu.VMEM((3 * BS, width * BS), BF16), pltpu.VMEM((3 * BS, width * BS), BF16)],
        compiler_params=pltpu.CompilerParams(vmem_limit_bytes=40 * 1024 * 1024),
    )(u, blocks, index)


GROUPS = len(TILES) * BS // 8
HALF = GROUPS // 2
PARTS = ((0, 128, "xyz"), (128, 128, "yxz"), (256, 32, "zx"))
SIZES = {"x": X, "y": 4, "z": Z}


def sum_copies():
    total = 2 * len(PARTS)
    for _, _, order in PARTS:
        total += 2 * sum(SIZES[axis] - 1 for axis in order)
    return total + SIZES["y"] - 1


def sum_kernel(g_ref, res, acc, other, bufs, ring, send_sem, recv_sem):
    d, l = lax.axis_index("depth"), lax.axis_index("lat")
    x, z, c = l // (2 * Z), lax.rem(l // 2, Z), lax.rem(l, 2)
    place = {"x": x, "y": d, "z": z}

    def device(axis, index):
        if axis == "y":
            return (index, l)
        if axis == "x":
            return (d, (index * Z + z) * 2 + c)
        return (d, (x * Z + index) * 2 + c)

    twin = (d, l + 1 - 2 * c)
    barrier = pltpu.get_barrier_semaphore()
    greeted = 1
    pl.semaphore_signal(barrier, inc=1, device_id=twin, device_id_type=MESH)
    for axis in "xyz":
        for off in range(1, SIZES[axis]):
            peer = device(axis, lax.rem(place[axis] + off, SIZES[axis]))
            pl.semaphore_signal(barrier, inc=1, device_id=peer, device_id_type=MESH)
            greeted += 1
    pl.semaphore_wait(barrier, greeted)

    used = [0]
    started = []

    def start(src, dst, peer):
        at = used[0]
        used[0] += 1
        copy = pltpu.make_async_remote_copy(
            src_ref=src, dst_ref=dst, send_sem=send_sem.at[at], recv_sem=recv_sem.at[at],
            device_id=peer, device_id_type=MESH,
        )
        copy.start()
        started.append(copy)
        return copy

    mine, theirs = c * HALF, (1 - c) * HALF
    arriving = [start(g_ref.at[pl.ds(theirs + at, n)], other.at[pl.ds(at, n)], twin) for at, n, _ in PARTS]
    state = []
    slot = [0]

    def scatter(part):
        base, n, order, phase = part["base"], part["n"], part["order"], part["phase"]
        axis = order[phase]
        k = SIZES[axis]
        piece = n // k
        here = place[axis]
        copies = []
        for off in range(1, k):
            to = lax.rem(here + off, k)
            room = bufs.at[pl.ds(slot[0], piece)]
            copies.append((start(acc.at[pl.ds(base + to * piece, piece)], room, device(axis, to)), slot[0]))
            slot[0] += piece
        part["wait"] = copies
        part["base"], part["n"], part["phase"] = base + here * piece, piece, phase + 1
        part["path"].append((axis, part["base"], piece))

    def collect(part):
        own = pl.ds(part["base"], part["n"])
        value = acc[own]
        for copy, at in part["wait"]:
            copy.wait_recv()
            value = value + bufs[at : at + part["n"]]
        acc[own] = value

    for at, (copy, (base, n, order)) in enumerate(zip(arriving, PARTS)):
        copy.wait_recv()
        acc[base : base + n] = g_ref[pl.ds(mine + base, n)] + other[base : base + n]
        part = {"base": base, "n": n, "order": order, "phase": 0, "path": []}
        state.append(part)
        scatter(part)
    for phase in range(3):
        for part in state:
            if phase < len(part["order"]):
                collect(part)
                if phase + 1 < len(part["order"]):
                    scatter(part)
    last = state[-1]
    own = pl.ds(last["base"], last["n"])
    ring[d] = acc[own]
    copies = []
    for off in range(1, SIZES["y"]):
        to = lax.rem(d + off, SIZES["y"])
        copies.append(start(acc.at[own], ring.at[d], device("y", to)))
    for copy in copies:
        copy.wait_recv()
    value = ring[0]
    for at in range(1, SIZES["y"]):
        value = value + ring[at]
    res[pl.ds(mine + last["base"], last["n"])] = value
    for part in state[:-1]:
        res[pl.ds(mine + part["base"], part["n"])] = acc[pl.ds(part["base"], part["n"])]

    def gather(part):
        axis, base, n = part["path"][-1]
        part["path"].pop()
        k = SIZES[axis]
        here = place[axis]
        region = res.at[pl.ds(mine + base, n)]
        part["wait"] = []
        for off in range(1, k):
            to = lax.rem(here + off, k)
            part["wait"].append(start(region, region, device(axis, to)))

    for part in state:
        gather(part)
    for _ in range(3):
        for part in state:
            if part["wait"] is None:
                continue
            for copy in part["wait"]:
                copy.wait_recv()
            if part["path"]:
                gather(part)
            else:
                part["wait"] = None
    finals = []
    for base, n, _ in PARTS:
        region = res.at[pl.ds(mine + base, n)]
        finals.append(start(region, region, twin))
    for copy in finals:
        copy.wait_recv()
    for copy in started:
        copy.wait_send()


def sum_everywhere(g):
    copies = sum_copies()
    room = 0
    for _, n, order in PARTS:
        for axis in order:
            n //= SIZES[axis]
            room += (SIZES[axis] - 1) * n
    return pl.pallas_call(
        sum_kernel,
        out_shape=jax.ShapeDtypeStruct((GROUPS, 8, BS), F32),
        in_specs=[VMEM],
        out_specs=VMEM,
        scratch_shapes=[
            pltpu.VMEM((HALF, 8, BS), F32),
            pltpu.VMEM((HALF, 8, BS), F32),
            pltpu.VMEM((room, 8, BS), F32),
            pltpu.VMEM((SIZES["y"], 1, 8, BS), F32),
            pltpu.SemaphoreType.DMA((copies,)),
            pltpu.SemaphoreType.DMA((copies,)),
        ],
        compiler_params=pltpu.CompilerParams(
            collective_id=8, has_side_effects=True, vmem_limit_bytes=40 * 1024 * 1024
        ),
    )(g.reshape(GROUPS, 8, BS))


def tip_kernel(s_ref, tip_ref, out_ref):
    i = pl.program_id(0)
    for j in range(MB):
        cols = slice(j * BS, (j + 1) * BS)

        @pl.when(j <= i)
        def _():
            out_ref[:, cols] = tip_ref[:, cols] - s_ref[i * (i + 1) // 2 + j]

        @pl.when(j > i)
        def _():
            out_ref[:, cols] = tip_ref[:, cols] - s_ref[j * (j + 1) // 2 + i].T


def finish_tip(total, tip):
    n = tip.shape[0]
    return pl.pallas_call(
        tip_kernel,
        grid=(MB,),
        out_shape=jax.ShapeDtypeStruct(tip.shape, F32),
        in_specs=[
            pl.BlockSpec((len(TILES), BS, BS), lambda i: (0, 0, 0)),
            pl.BlockSpec((BS, n), lambda i: (i, 0)),
        ],
        out_specs=pl.BlockSpec((BS, n), lambda i: (i, 0)),
        compiler_params=pltpu.CompilerParams(vmem_limit_bytes=40 * 1024 * 1024),
    )(total.reshape(len(TILES), BS, BS), tip)


def body(diag_blocks, coupling, offsets, arrow_blocks, arrow_index, tip):
    layers = lax.axis_size("depth")
    own = diag_blocks[0]
    incoming = jnp.zeros_like(own)
    for step in range(layers):
        u = factorize(own, incoming)
        handed, incoming = exchange(u, coupling[0], offsets[0], step)
    terms, lower = arrow_terms(u, arrow_blocks[0], arrow_index[0])
    schur_tip = finish_tip(sum_everywhere(terms), tip)
    return (lower[None], handed[None], schur_tip)


def solution(mesh):
    return jax.shard_map(
        body,
        mesh=mesh,
        in_specs=(
            P("depth", "lat", None, None),
            P("depth", "lat", None, None, None),
            P("depth", "lat", None),
            P("depth", "lat", None, None, None),
            P("depth", "lat", None),
            P(),
        ),
        out_specs=(P("depth", "lat", None, None), P("depth", "lat", None, None), P()),
        check_vma=False,
    )
```

```python
import functools

import jax
import jax.numpy as jnp
from jax import lax
from jax.experimental import pallas as pl
from jax.experimental.pallas import tpu as pltpu
from jax.sharding import PartitionSpec as P

BS = 128
PANEL = 32
PANELS = BS // PANEL
REACH = 8
MB = 8
F32 = jnp.float32
BF16 = jnp.bfloat16
MESH = pl.DeviceIdType.MESH
X, Z = 4, 8
SIZES = {"x": X, "y": 4, "z": Z}
HALF_TILES = 18
HALF = HALF_TILES * 16
PARTS = ((0, 128, "xyz"), (128, 128, "yxz"), (256, 32, "zx"))
TOP = 4


def split2(x):
    high = x.astype(BF16)
    return high, (x - high.astype(F32)).astype(BF16)


def split3(x):
    high = x.astype(BF16)
    rest = x - high.astype(F32)
    middle = rest.astype(BF16)
    return high, middle, (rest - middle.astype(F32)).astype(BF16)


def dot(a, b):
    return jnp.dot(a, b, preferred_element_type=F32)


def dot_t(a, b):
    return lax.dot_general(a, b, (((0,), (0,)), ((), ())), preferred_element_type=F32)


def gram_exact(u, v):
    uh, um, ul = split3(u)
    vh, vm, vl = split3(v)
    return dot_t(
        jnp.concatenate([uh, uh, uh, um, um, ul], 0),
        jnp.concatenate([vh, vm, vl, vh, vm, vh], 0),
    )


def eliminate(part, j0):
    count = part[0].shape[0]
    shape = (count, 8, BS)
    lane = lax.broadcasted_iota(jnp.int32, shape, 2)
    sub = lax.broadcasted_iota(jnp.int32, shape, 1)
    groups = len(part)
    spread = lambda x: jnp.broadcast_to(x, shape)
    for g in range(groups):
        c0 = j0 + 8 * g
        cols = [[spread(part[v][:, :, c0 + k : c0 + k + 1]) for k in range(8)] for v in range(g, groups)]
        keep = (lane < c0) | (lane >= c0 + 8)
        x = jnp.where(keep, part[g], jnp.where(lane == c0 + sub, 1.0, 0.0))
        d = cols[0]
        scales, rows, low = [], [], {}
        for i in range(8):
            scale = lax.rsqrt(spread(d[i][:, i : i + 1, :]))
            li = d[i] * scale
            for k in range(i + 1, 8):
                low[k, i] = spread(li[:, k : k + 1, :])
                d[k] = d[k] - li * low[k, i]
            row = spread(x[:, i : i + 1, :]) * scale
            scales.append(scale)
            rows.append(row)
            x = jnp.where(sub > i, x - li * row, jnp.where(sub == i, row, x))
        for k in range(1, 8):
            for i in range(k):
                x = jnp.where((sub == i) & (lane == c0 + k), low[k, i], x)
        part[g] = x
        for v in range(g + 1, groups):
            d = cols[v - g]
            x = jnp.where(keep, part[v], 0.0)
            for i in range(8):
                mi = d[i] * scales[i]
                for k in range(i + 1, 8):
                    d[k] = d[k] - mi * low[k, i]
                x = x - mi * rows[i]
            part[v] = x
    return jnp.concatenate(part, 1)


def kernel(
    diag_hbm, coup_hbm, off_ref, arrow_hbm, idx_ref, tip_hbm,
    lower_ref, handed_ref, out_ref,
    dbuf, cbuf, bbuf, tbuf, ubuf, corr, landed, window, wide, cwide, bwide, stacked, early, placed, hi, lo,
    g_ref, other, acc, bufs, ring, res,
    load_sem, win_send, win_recv, dep_send, dep_recv, sum_send, sum_recv,
):
    depths, lats = lax.axis_size("depth"), lax.axis_size("lat")
    d, l = lax.axis_index("depth"), lax.axis_index("lat")
    count, width = off_ref.shape
    spokes = idx_ref.shape[1]
    px, pz, c = l // (2 * Z), lax.rem(l // 2, Z), lax.rem(l, 2)
    place = {"x": px, "y": d, "z": pz}
    twin = (d, l + 1 - 2 * c)

    def device(axis, index):
        if axis == "y":
            return (index, l)
        if axis == "x":
            return (d, (index * Z + pz) * 2 + c)
        return (d, (px * Z + index) * 2 + c)

    def lat_at(step):
        return (d, lax.rem(l + step + lats, lats))

    def remote(src, dst, send, recv, peer):
        return pltpu.make_async_remote_copy(
            src_ref=src, dst_ref=dst, send_sem=send, recv_sem=recv, device_id=peer, device_id_type=MESH
        )

    loads = [
        pltpu.make_async_copy(src, dst, load_sem.at[at])
        for at, (src, dst) in enumerate(((diag_hbm, dbuf), (coup_hbm, cbuf), (arrow_hbm, bbuf), (tip_hbm, tbuf)))
    ]
    for load in loads:
        load.start()

    barrier = pltpu.get_barrier_semaphore()
    greeted = 0
    peers = [twin, lat_at(-2), lat_at(2)]
    for axis in "xyz":
        peers += [device(axis, lax.rem(place[axis] + off, SIZES[axis])) for off in range(1, SIZES[axis])]
    for peer in peers:
        pl.semaphore_signal(barrier, inc=1, device_id=peer, device_id_type=MESH)

    def prepare():
        def couple(at, _):
            ch, cl = split2(cbuf[at])
            cwide[at] = jnp.concatenate([ch, ch, cl], 0)
            return 0

        def spoke(n, _):
            for s in range(spokes):
                bh, bl = split2(bbuf[n, s])
                bwide[n, :, s * BS : (s + 1) * BS] = jnp.concatenate([bh, bh, bl], 0)
            placed[n, spokes] = jnp.zeros(placed.shape[2:], BF16)
            return 0

        loads[1].wait()
        loads[2].wait()
        lax.fori_loop(0, count * width, couple, 0)
        lax.fori_loop(0, count, spoke, 0)

    def handed_copy(at):
        if at < TOP:
            rows = (at, pl.ds(0, 2 * PANEL))
        else:
            rows = (slice(None), pl.ds((at - TOP + 2) * PANEL, PANEL))
        return remote(
            handed_ref.at[rows], landed.at[rows], dep_send.at[at], dep_recv.at[at],
            (lax.rem(d + 1, depths), l),
        )

    @pl.when(d == 0)
    def _():
        landed[...] = jnp.zeros_like(landed)

    loads[0].wait()
    pl.semaphore_wait(barrier, len(peers))

    @pl.when(d > 0)
    def _():
        prepare()

    def panel_rows(p):
        return pl.ds(p * PANEL, PANEL)

    def panel_copies(p):
        own = window.at[pl.ds(REACH, count), panel_rows(p)]

        def to(first):
            return window.at[pl.ds(first, count), panel_rows(p)]

        return (
            remote(own, to(4 * count), win_send.at[p, 0], win_recv.at[p, 0], lat_at(-2)),
            remote(own, to(0), win_send.at[p, 1], win_recv.at[p, 1], lat_at(2)),
            remote(own, to(count + 2 * count * c), win_send.at[p, 2], win_recv.at[p, 2], twin),
        )

    def forward_copy(p):
        src = window.at[pl.ds(4 * count - 4 * count * c, count), panel_rows(p)]
        dst = window.at[pl.ds(3 * count - 2 * count * c, count), panel_rows(p)]
        return remote(src, dst, win_send.at[p, 3], win_recv.at[p, 3], twin)

    def forward(p):
        remote(
            window.at[pl.ds(REACH, count), panel_rows(p)],
            window.at[pl.ds(4 * count - 4 * count * c, count), panel_rows(p)],
            win_send.at[p, c], win_recv.at[p, c], twin,
        ).wait_recv()
        forward_copy(p).start()

    def wait_panel(p):
        remote(
            window.at[pl.ds(REACH, count), panel_rows(p)],
            window.at[pl.ds(4 * count * c, count), panel_rows(p)],
            win_send.at[p, 1 - c], win_recv.at[p, 1 - c], twin,
        ).wait_recv()
        panel_copies(p)[2].wait_recv()
        forward_copy(p).wait_recv()

    for p in range(PANELS):
        j0, end = p * PANEL, (p + 1) * PANEL
        needed = {0: range(TOP), 2: (TOP,), 3: (TOP + 1,)}.get(p, ())
        if needed:

            @pl.when(d > 0)
            def _():
                for at in needed:
                    handed_copy(at).wait_recv()

        a = dbuf[:, j0:end, :] + landed[:, j0:end, :]
        lane = lax.broadcasted_iota(jnp.int32, a.shape, 2)
        row = j0 + lax.broadcasted_iota(jnp.int32, a.shape, 1)
        if p:
            a = jnp.where(lane < j0, 0.0, a) - corr[:, j0:end, :]
        u = eliminate([a[:, 8 * v : 8 * v + 8] for v in range(PANEL // 8)], j0)
        ubuf[:, j0:end, :] = u
        window[REACH : REACH + count, j0:end, :] = jnp.where(lane <= row, u, 0.0)
        for copy in panel_copies(p):
            copy.start()
        if end < BS:
            right = jnp.where((lane < end) & (lane > row), 0.0, u)
            for m in range(count):
                full = gram_exact(u[m], right[m])[end:]
                if p:
                    old = corr[m, end:, :]
                    ln = lax.broadcasted_iota(jnp.int32, old.shape, 1)
                    full = full + jnp.where((ln >= j0) & (ln < end), 0.0, old)
                corr[m, end:, :] = full
        if p == 2:
            forward(0)

    def update(ranges, hand_on):
        forward(1)
        arrived = 0
        for stage, (first, last) in enumerate(ranges):
            if last == 2 * PANEL:
                pass
            elif arrived < 3:
                forward(2)
                forward(3)
                arrived = 3
            for p in range(first // PANEL, last // PANEL):
                wait_panel(p)
            rows = last - first
            for step in range(-2, 3):
                at = REACH + step * count
                inside = (l + step >= 0) & (l + step < lats)
                high, low = split2(jnp.where(inside, window[at : at + count, first:last, :], 0.0))
                wide[at : at + count, first:last, :] = jnp.concatenate([high, low, high], 2)
            for m in range(count):
                for w in range(width):
                    x = dot(wide[off_ref[m, w] + (m + REACH), first:last, :], cwide[m * width + w])
                    xh, xl = split2(x)
                    stacked[w * rows : (w + 1) * rows, :] = jnp.concatenate([xh, xl], 1)
                both = dot_t(stacked[: width * rows, :BS], stacked[: width * rows, :])
                if stage:
                    both = both + early[m]
                if stage + 1 < len(ranges):
                    early[m] = both
                else:
                    cross = both[:, BS:]
                    handed_ref[m] = -(both[:, :BS] + cross + cross.T)
                    if hand_on:
                        handed_copy(m).start()
        if hand_on:
            handed_copy(TOP).start()
            handed_copy(TOP + 1).start()

    @pl.when(d == 0)
    def _():
        prepare()

    @pl.when(d < depths - 1)
    def _():
        update(((0, 2 * PANEL), (2 * PANEL, 3 * PANEL), (3 * PANEL, BS)), True)

    row = lax.broadcasted_iota(jnp.int32, (BS, BS), 0)
    col = lax.broadcasted_iota(jnp.int32, (BS, BS), 1)
    for n in range(count):
        high, low = split2(jnp.where(col <= row, ubuf[n], 0.0))
        t = dot(jnp.concatenate([high, low, high], 1), bwide[n])
        for s in range(spokes):
            th, tl = split2(t[:, s * BS : (s + 1) * BS])
            placed[n, s, 0] = th
            placed[n, s, 1] = tl
    for n in range(count):
        for m in range(MB):
            slot = spokes
            for s in range(spokes):
                slot = jnp.where(idx_ref[n, s] == m, s, slot)
            both = placed[n, slot]
            for at in (m, m + MB)[: 2 if m < MB // 2 else 1]:
                hi[n * BS : (n + 1) * BS, at * BS : (at + 1) * BS] = both[0]
                lo[n * BS : (n + 1) * BS, at * BS : (at + 1) * BS] = both[1]

    def tile_product(i, first, tiles):
        left = pl.ds(pl.multiple_of(i * BS, BS), BS)
        right = pl.ds(pl.multiple_of(first * BS, BS), tiles * BS)
        return dot_t(hi[:, left], hi[:, right]) + dot_t(hi[:, left], lo[:, right]) + dot_t(lo[:, left], hi[:, right])

    def put(h, k, value):
        g_ref[pl.ds((h * HALF_TILES + k) * 16, 16)] = value.reshape(16, 8, BS)

    def half_products(h):
        for ii in range(4):
            product = tile_product(4 * h + ii, 4 * h + ii, 4)
            for delta in range(4):
                put(h, delta * 4 + ii, product[:, delta * BS : (delta + 1) * BS])
        for ii in range(2):
            put(h, 16 + ii, tile_product(2 * h + ii, 2 * h + ii + 4, 1))

    used = [0]
    started = []

    def start(src, dst, peer):
        at = used[0]
        used[0] += 1
        copy = remote(src, dst, sum_send.at[at], sum_recv.at[at], peer)
        copy.start()
        started.append(copy)
        return copy

    mine, theirs = c * HALF, (1 - c) * HALF
    half_products(1 - c)
    arriving = [start(g_ref.at[pl.ds(theirs + at, n)], other.at[pl.ds(at, n)], twin) for at, n, _ in PARTS]
    half_products(c)
    slot = [0]

    def scatter(part):
        axis = part["order"][part["phase"]]
        k, here = SIZES[axis], place[axis]
        base, piece = part["base"], part["n"] // k
        part["wait"] = []
        for off in range(1, k):
            to = lax.rem(here + off, k)
            copy = start(
                acc.at[pl.ds(base + to * piece, piece)], bufs.at[pl.ds(slot[0], piece)], device(axis, to)
            )
            part["wait"].append((copy, slot[0]))
            slot[0] += piece
        part["base"], part["n"], part["phase"] = base + here * piece, piece, part["phase"] + 1
        part["path"].append((axis, part["base"], piece))

    def collect(part):
        own = pl.ds(part["base"], part["n"])
        value = acc[own]
        for copy, at in part["wait"]:
            copy.wait_recv()
            value = value + bufs[at : at + part["n"]]
        acc[own] = value

    state = []
    for copy, (base, n, order) in zip(arriving, PARTS):
        copy.wait_recv()
        acc[base : base + n] = g_ref[pl.ds(mine + base, n)] + other[base : base + n]
        part = {"base": base, "n": n, "order": order, "phase": 0, "path": []}
        state.append(part)
        scatter(part)

    for n in range(count):
        u = ubuf[n]
        lower_ref[n] = jnp.where(col > row, u, jnp.where(col == row, 1.0 / u, 0.0)).T

    @pl.when(d == depths - 1)
    def _():
        update(((0, BS),), False)

    for phase in range(3):
        for part in state:
            if phase < len(part["order"]):
                collect(part)
                if phase + 1 < len(part["order"]):
                    scatter(part)
    last = state[-1]
    own = pl.ds(last["base"], last["n"])
    ring[d] = acc[own]
    copies = []
    for off in range(1, SIZES["y"]):
        to = lax.rem(d + off, SIZES["y"])
        copies.append(start(acc.at[own], ring.at[d], device("y", to)))
    for part in state[:-1]:
        res[pl.ds(mine + part["base"], part["n"])] = acc[pl.ds(part["base"], part["n"])]

    def gather(part):
        axis, base, n = part["path"].pop()
        k, here = SIZES[axis], place[axis]
        region = res.at[pl.ds(mine + base, n)]
        part["wait"] = [start(region, region, device(axis, lax.rem(here + off, k))) for off in range(1, k)]

    for part in state[:-1]:
        gather(part)
    for copy in copies:
        copy.wait_recv()
    value = ring[0]
    for at in range(1, SIZES["y"]):
        value = value + ring[at]
    res[pl.ds(mine + last["base"], last["n"])] = value
    gather(last)

    def emit(h, first, tiles):
        def one(k, _):
            i = jnp.where(k < 16, 4 * h + lax.rem(k, 4), 2 * h + k - 16)
            j = lax.rem(i + k // 4, MB)
            rows, cols = pl.ds(pl.multiple_of(i * BS, BS), BS), pl.ds(pl.multiple_of(j * BS, BS), BS)
            value = res[pl.ds((h * HALF_TILES + k) * 16, 16)].reshape(BS, BS)
            out_ref[rows, cols] = tbuf[rows, cols] - value

            @pl.when(k >= 4)
            def _():
                out_ref[cols, rows] = tbuf[cols, rows] - value.T

            return 0

        lax.fori_loop(first, first + tiles, one, 0)

    finals = []
    for _ in range(3):
        for part, (base, n, _) in zip(state, PARTS):
            if part["wait"] is None:
                continue
            for copy in part["wait"]:
                copy.wait_recv()
            if part["path"]:
                gather(part)
            else:
                part["wait"] = None
                region = res.at[pl.ds(mine + base, n)]
                finals.append((start(region, region, twin), base // 16, n // 16))
    loads[3].wait()
    for _, first, tiles in finals:
        emit(c, first, tiles)
    for copy, first, tiles in finals:
        copy.wait_recv()
        emit(1 - c, first, tiles)

    for copy in started:
        copy.wait_send()
    for p in range(PANELS):
        for copy in panel_copies(p):
            copy.wait_send()
        forward_copy(p).wait_send()

    @pl.when(d < depths - 1)
    def _():
        for at in range(TOP + 2):
            handed_copy(at).wait_send()


def body(diag_blocks, coupling, offsets, arrow_blocks, arrow_index, tip):
    count, width = offsets.shape[1:]
    spokes = arrow_index.shape[2]
    copies, room = 2 * len(PARTS) + SIZES["y"] - 1, 0
    for _, n, order in PARTS:
        for axis in order:
            n //= SIZES[axis]
            room += (SIZES[axis] - 1) * n
            copies += 2 * (SIZES[axis] - 1)
    vmem, smem, hbm = (pl.BlockSpec(memory_space=space) for space in (pltpu.VMEM, pltpu.SMEM, pl.ANY))
    blocks = jax.ShapeDtypeStruct((count, BS, BS), F32)
    band = 2 * REACH + count
    dma = pltpu.SemaphoreType.DMA
    lower, handed, schur_tip = pl.pallas_call(
        kernel,
        out_shape=(blocks, blocks, jax.ShapeDtypeStruct(tip.shape, F32)),
        in_specs=[hbm, hbm, smem, hbm, smem, hbm],
        out_specs=(vmem, vmem, vmem),
        scratch_shapes=[
            pltpu.VMEM((count, BS, BS), F32),
            pltpu.VMEM((count * width, BS, BS), F32),
            pltpu.VMEM((count, spokes, BS, BS), F32),
            pltpu.VMEM(tip.shape, F32),
            pltpu.VMEM((count, BS, BS), F32),
            pltpu.VMEM((count, BS, BS), F32),
            pltpu.VMEM((count, BS, BS), F32),
            pltpu.VMEM((band, BS, BS), F32),
            pltpu.VMEM((band, BS, 3 * BS), BF16),
            pltpu.VMEM((count * width, 3 * BS, BS), BF16),
            pltpu.VMEM((count, 3 * BS, spokes * BS), BF16),
            pltpu.VMEM((width * BS, 2 * BS), BF16),
            pltpu.VMEM((count, BS, 2 * BS), F32),
            pltpu.VMEM((count, spokes + 1, 2, BS, BS), BF16),
            pltpu.VMEM((count * BS, 12 * BS), BF16),
            pltpu.VMEM((count * BS, 12 * BS), BF16),
            pltpu.VMEM((2 * HALF, 8, BS), F32),
            pltpu.VMEM((HALF, 8, BS), F32),
            pltpu.VMEM((HALF, 8, BS), F32),
            pltpu.VMEM((room, 8, BS), F32),
            pltpu.VMEM((SIZES["y"], 1, 8, BS), F32),
            pltpu.VMEM((2 * HALF, 8, BS), F32),
            dma((4,)),
            dma((PANELS, 4)),
            dma((PANELS, 4)),
            dma((TOP + 2,)),
            dma((TOP + 2,)),
            dma((copies,)),
            dma((copies,)),
        ],
        compiler_params=pltpu.CompilerParams(
            collective_id=0, has_side_effects=True, vmem_limit_bytes=56 * 1024 * 1024
        ),
    )(diag_blocks[0], coupling[0].reshape(count * width, BS, BS), offsets[0], arrow_blocks[0], arrow_index[0], tip)
    return (lower[None], handed[None], schur_tip)


def solution(mesh):
    return jax.shard_map(
        body,
        mesh=mesh,
        in_specs=(
            P("depth", "lat", None, None),
            P("depth", "lat", None, None, None),
            P("depth", "lat", None),
            P("depth", "lat", None, None, None),
            P("depth", "lat", None),
            P(),
        ),
        out_specs=(P("depth", "lat", None, None), P("depth", "lat", None, None), P()),
        check_vma=False,
    )
```

```python
import functools

import jax
import jax.numpy as jnp
from jax import lax
from jax.experimental import pallas as pl
from jax.experimental.pallas import tpu as pltpu
from jax.sharding import PartitionSpec as P

BS = 128
PANEL = 32
PANELS = BS // PANEL
REACH = 8
MB = 8
F32 = jnp.float32
BF16 = jnp.bfloat16
MESH = pl.DeviceIdType.MESH
X, Z = 4, 8
SIZES = {"x": X, "y": 4, "z": Z}
HALF_TILES = 18
HALF = HALF_TILES * 16
PARTS = ((0, 128, "xyz"), (128, 128, "yxz"), (256, 32, "zx"))
PIECES = ((64, 0, 2, 0, 32), (80, 1, 4, 0, 16), (96, 1, 4, 16, 32), (112, 2, 4, 0, 16), (128, 2, 4, 16, 32))
RELAYED = 3


def split2(x):
    high = x.astype(BF16)
    return high, (x - high.astype(F32)).astype(BF16)


def split3(x):
    high = x.astype(BF16)
    rest = x - high.astype(F32)
    middle = rest.astype(BF16)
    return high, middle, (rest - middle.astype(F32)).astype(BF16)


def dot(a, b):
    return jnp.dot(a, b, preferred_element_type=F32)


def dot_t(a, b):
    return lax.dot_general(a, b, (((0,), (0,)), ((), ())), preferred_element_type=F32)


def gram_exact(u, v):
    uh, um, ul = split3(u)
    vh, vm, vl = split3(v)
    return dot_t(
        jnp.concatenate([uh, uh, uh, um, um, ul], 0),
        jnp.concatenate([vh, vm, vl, vh, vm, vh], 0),
    )


def eliminate(part, j0, done):
    count = part[0].shape[0]
    shape = (count, 8, BS)
    lane = lax.broadcasted_iota(jnp.int32, shape, 2)
    sub = lax.broadcasted_iota(jnp.int32, shape, 1)
    groups = len(part)
    spread = lambda x: jnp.broadcast_to(x, shape)
    for g in range(groups):
        c0 = j0 + 8 * g
        cols = [[spread(part[v][:, :, c0 + k : c0 + k + 1]) for k in range(8)] for v in range(g, groups)]
        keep = (lane < c0) | (lane >= c0 + 8)
        x = jnp.where(keep, part[g], jnp.where(lane == c0 + sub, 1.0, 0.0))
        d = cols[0]
        scales, rows, low = [], [], {}
        for i in range(8):
            scale = lax.rsqrt(spread(d[i][:, i : i + 1, :]))
            li = d[i] * scale
            for k in range(i + 1, 8):
                low[k, i] = spread(li[:, k : k + 1, :])
                d[k] = d[k] - li * low[k, i]
            row = spread(x[:, i : i + 1, :]) * scale
            scales.append(scale)
            rows.append(row)
            x = jnp.where(sub > i, x - li * row, jnp.where(sub == i, row, x))
        for k in range(1, 8):
            for i in range(k):
                x = jnp.where((sub == i) & (lane == c0 + k), low[k, i], x)
        part[g] = x
        for v in range(g + 1, groups):
            d = cols[v - g]
            x = jnp.where(keep, part[v], 0.0)
            for i in range(8):
                mi = d[i] * scales[i]
                for k in range(i + 1, 8):
                    d[k] = d[k] - mi * low[k, i]
                x = x - mi * rows[i]
            part[v] = x
        done(g)


def kernel(
    diag_hbm, coup_hbm, off_ref, arrow_hbm, idx_ref,
    ubuf, handed_ref, res_hbm,
    dbuf, cbuf, bbuf, corr, landed, halves, thirds, fourths, wide, cwide, bwide, stacked, early, placed, hi, lo,
    g_ref, other, acc, bufs, ring, res,
    load_sem, store_sem, win_send, win_recv, dep_send, dep_recv, sum_send, sum_recv,
):
    depths, lats = lax.axis_size("depth"), lax.axis_size("lat")
    d, l = lax.axis_index("depth"), lax.axis_index("lat")
    count, width = off_ref.shape
    spokes = idx_ref.shape[1]
    px, pz, c = l // (2 * Z), lax.rem(l // 2, Z), lax.rem(l, 2)
    place = {"x": px, "y": d, "z": pz}
    twin = (d, l + 1 - 2 * c)

    def device(axis, index):
        if axis == "y":
            return (index, l)
        if axis == "x":
            return (d, (index * Z + pz) * 2 + c)
        return (d, (px * Z + index) * 2 + c)

    def lat_at(step):
        return (d, lax.rem(l + step + lats, lats))

    def remote(src, dst, send, recv, peer):
        return pltpu.make_async_remote_copy(
            src_ref=src, dst_ref=dst, send_sem=send, recv_sem=recv, device_id=peer, device_id_type=MESH
        )

    loads = [
        pltpu.make_async_copy(src, dst, load_sem.at[at])
        for at, (src, dst) in enumerate(((diag_hbm, dbuf), (coup_hbm, cbuf), (arrow_hbm, bbuf)))
    ]
    for load in loads:
        load.start()

    barrier = pltpu.get_barrier_semaphore()
    peers = [twin, lat_at(-2), lat_at(2), lat_at(2 * c - 1)]
    for axis in "xyz":
        peers += [device(axis, lax.rem(place[axis] + off, SIZES[axis])) for off in range(1, SIZES[axis])]
    for peer in peers:
        pl.semaphore_signal(barrier, inc=1, device_id=peer, device_id_type=MESH)

    def prepare():
        def couple(at, _):
            ch, cl = split2(cbuf[at])
            cwide[at] = jnp.concatenate([ch, ch, cl], 0)
            return 0

        def spoke(n, _):
            for s in range(spokes):
                bh, bl = split2(bbuf[n, s])
                bwide[n, :, s * BS : (s + 1) * BS] = jnp.concatenate([bh, bh, bl], 0)
            placed[n, spokes] = jnp.zeros(placed.shape[2:], BF16)
            return 0

        loads[1].wait()
        loads[2].wait()
        lax.fori_loop(0, count * width, couple, 0)
        lax.fori_loop(0, count, spoke, 0)

    def handed_copy(at):
        if at < count:
            rows = (at, pl.ds(0, PANEL))
        else:
            rows = (slice(None), pl.ds((at - count + 1) * PANEL, PANEL))
        return remote(
            handed_ref.at[rows], landed.at[rows], dep_send.at[at], dep_recv.at[at],
            (lax.rem(d + 1, depths), l),
        )

    @pl.when(d == 0)
    def _():
        landed[...] = jnp.zeros_like(landed)

    loads[0].wait()

    @pl.when(d > 0)
    def _():
        prepare()

    arrived = (halves, thirds, fourths)

    def place_of(step, p):
        _, buffer, blocks, first, last = PIECES[p]
        return arrived[buffer].at[pl.ds(step * blocks, blocks), pl.ds(first, last - first)]

    def received(p, at, step):
        return remote(place_of(2, p), place_of(step, p), win_send.at[p, at], win_recv.at[p, at], twin)

    def piece_copies(p):
        own = place_of(2, p)
        copies = [
            remote(own, place_of(4, p), win_send.at[p, 0], win_recv.at[p, 0], lat_at(-2)),
            remote(own, place_of(0, p), win_send.at[p, 1], win_recv.at[p, 1], lat_at(2)),
            remote(own, place_of(1 + 2 * c, p), win_send.at[p, 2], win_recv.at[p, 2], twin),
        ]
        if p >= RELAYED:
            copies.append(crossing(p))
        return copies

    def crossing(p):
        if p < RELAYED:
            src, peer = place_of(4 - 4 * c, p), twin
        else:
            src, peer = place_of(2, p), lat_at(2 * c - 1)
        return remote(src, place_of(3 - 2 * c, p), win_send.at[p, 3], win_recv.at[p, 3], peer)

    def hand_over(p):
        received(p, c, 4 - 4 * c).wait_recv()
        if p < RELAYED:
            crossing(p).start()

    def wait_piece(p):
        received(p, 1 - c, 4 * c).wait_recv()
        received(p, 2, 1 + 2 * c).wait_recv()
        crossing(p).wait_recv()

    def pack(p):
        end, buffer, blocks, first, last = PIECES[p]
        rows = end - (last - first)
        value = ubuf[:, rows:end, :]
        lane = lax.broadcasted_iota(jnp.int32, value.shape, 2)
        value = jnp.where(lane <= rows + lax.broadcasted_iota(jnp.int32, value.shape, 1), value, 0.0)
        if buffer == 0:
            half = lane[:2] < BS // 2
            value = jnp.where(half, value[:2], pltpu.roll(value[2:], BS // 2, 2))
        elif buffer == 1:
            top = ubuf[:, first:last, :]
            top = jnp.where(lane <= first + lax.broadcasted_iota(jnp.int32, top.shape, 1), top, 0.0)
            value = jnp.where(lane < BS - PANEL, value, pltpu.roll(top, BS - PANEL, 2))
        arrived[buffer][2 * blocks : 3 * blocks, first:last, :] = value

    def widen(rows, blocks, value):
        high, low = split2(value)
        wide[blocks, rows, :] = jnp.concatenate([high, low, high], 2)

    def unpack(buffers):
        for step in range(5):
            inside = (l + step >= 2) & (l + step < lats + 2)
            at = step * count
            for buffer in buffers:
                blocks = 2 if buffer == 0 else count
                value = jnp.where(inside, arrived[buffer][step * blocks : (step + 1) * blocks], 0.0)
                lane = lax.broadcasted_iota(jnp.int32, value.shape, 2)
                if buffer == 0:
                    half = lane < BS // 2
                    widen(slice(32, 64), slice(at, at + 2), jnp.where(half, value, 0.0))
                    widen(slice(32, 64), slice(at + 2, at + 4), jnp.where(half, pltpu.roll(value, BS // 2, 2), 0.0))
                elif buffer == 1:
                    widen(slice(64, 96), slice(at, at + count), jnp.where(lane < BS - PANEL, value, 0.0))
                    top = jnp.where(lane < PANEL, pltpu.roll(value, PANEL, 2), 0.0)
                    widen(slice(0, 32), slice(at, at + count), top)
                else:
                    widen(slice(96, 128), slice(at, at + count), value)

    for p in range(PANELS):
        j0, end = p * PANEL, (p + 1) * PANEL
        needed = (count + p - 1,) if p else range(count)

        @pl.when(d > 0)
        def _():
            for at in needed:
                handed_copy(at).wait_recv()

        a = dbuf[:, j0:end, :] + landed[:, j0:end, :]
        lane = lax.broadcasted_iota(jnp.int32, a.shape, 2)
        row = j0 + lax.broadcasted_iota(jnp.int32, a.shape, 1)
        if p:
            a = jnp.where(lane < j0, 0.0, a) - corr[:, j0:end, :]
        part = [a[:, 8 * v : 8 * v + 8] for v in range(PANEL // 8)]

        def done(g):
            if g % 2 == 0:
                return
            row = j0 + 8 * g - 8
            ubuf[:, row : row + 16, :] = jnp.concatenate(part[g - 1 : g + 1], 1)
            for at, piece in enumerate(PIECES):
                if piece[0] == row + 16:
                    pack(at)
                    if at == 0:
                        pl.semaphore_wait(barrier, len(peers))
                    for copy in piece_copies(at):
                        copy.start()
            if row + 16 == PIECES[3][0]:
                hand_over(0)

        eliminate(part, j0, done)
        if end < BS:
            u = jnp.concatenate(part, 1)
            right = jnp.where((lane < end) & (lane > row), 0.0, u)
            for m in range(count):
                full = gram_exact(u[m], right[m])[end:]
                if p:
                    old = corr[m, end:, :]
                    ln = lax.broadcasted_iota(jnp.int32, old.shape, 1)
                    full = full + jnp.where((ln >= j0) & (ln < end), 0.0, old)
                corr[m, end:, :] = full

    def update(ranges, hand_on):
        for p in range(1, RELAYED):
            hand_over(p)
        for stage, (first, last) in enumerate(ranges):
            rows = last - first
            if first == 0:
                for p in range(RELAYED):
                    wait_piece(p)
                unpack((0, 1))
            if last == BS:
                for p in range(RELAYED, len(PIECES)):
                    hand_over(p)
                    wait_piece(p)
                unpack((2,))
            for m in range(count):
                for w in range(width):
                    x = dot(wide[off_ref[m, w] + (m + REACH), first:last, :], cwide[m * width + w])
                    xh, xl = split2(x)
                    stacked[w * rows : (w + 1) * rows, :] = jnp.concatenate([xh, xl], 1)
                both = dot_t(stacked[: width * rows, :BS], stacked[: width * rows, :])
                if stage:
                    both = both + early[m]
                if stage + 1 < len(ranges):
                    early[m] = both
                else:
                    cross = both[:, BS:]
                    handed_ref[m] = -(both[:, :BS] + cross + cross.T)
                    if hand_on:
                        handed_copy(m).start()
        if hand_on:
            for p in range(1, PANELS):
                handed_copy(count + p - 1).start()

    @pl.when(d == 0)
    def _():
        prepare()

    @pl.when(d < depths - 1)
    def _():
        update(((0, 96), (96, 128)), True)

    row = lax.broadcasted_iota(jnp.int32, (BS, BS), 0)
    col = lax.broadcasted_iota(jnp.int32, (BS, BS), 1)
    for n in range(count):
        high, low = split2(jnp.where(col <= row, ubuf[n], 0.0))
        t = dot(jnp.concatenate([high, low, high], 1), bwide[n])
        for s in range(spokes):
            th, tl = split2(t[:, s * BS : (s + 1) * BS])
            placed[n, s, 0] = th
            placed[n, s, 1] = tl
    for n in range(count):
        for m in range(MB):
            slot = spokes
            for s in range(spokes):
                slot = jnp.where(idx_ref[n, s] == m, s, slot)
            both = placed[n, slot]
            for at in (m, m + MB)[: 2 if m < MB // 2 else 1]:
                hi[n * BS : (n + 1) * BS, at * BS : (at + 1) * BS] = both[0]
                lo[n * BS : (n + 1) * BS, at * BS : (at + 1) * BS] = both[1]

    def tile_product(i, first, tiles):
        left = pl.ds(pl.multiple_of(i * BS, BS), BS)
        right = pl.ds(pl.multiple_of(first * BS, BS), tiles * BS)
        return dot_t(hi[:, left], hi[:, right]) + dot_t(hi[:, left], lo[:, right]) + dot_t(lo[:, left], hi[:, right])

    def put(h, k, value):
        g_ref[pl.ds((h * HALF_TILES + k) * 16, 16)] = value.reshape(16, 8, BS)

    def half_products(h):
        for ii in range(4):
            product = tile_product(4 * h + ii, 4 * h + ii, 4)
            for delta in range(4):
                put(h, delta * 4 + ii, product[:, delta * BS : (delta + 1) * BS])
        for ii in range(2):
            put(h, 16 + ii, tile_product(2 * h + ii, 2 * h + ii + 4, 1))

    used = [0]
    started = []

    def start(src, dst, peer):
        at = used[0]
        used[0] += 1
        copy = remote(src, dst, sum_send.at[at], sum_recv.at[at], peer)
        copy.start()
        started.append(copy)
        return copy

    mine, theirs = c * HALF, (1 - c) * HALF
    half_products(1 - c)
    arriving = [start(g_ref.at[pl.ds(theirs + at, n)], other.at[pl.ds(at, n)], twin) for at, n, _ in PARTS]
    half_products(c)
    slot = [0]

    def scatter(part):
        axis = part["order"][part["phase"]]
        k, here = SIZES[axis], place[axis]
        base, piece = part["base"], part["n"] // k
        part["wait"] = []
        for off in range(1, k):
            to = lax.rem(here + off, k)
            copy = start(
                acc.at[pl.ds(base + to * piece, piece)], bufs.at[pl.ds(slot[0], piece)], device(axis, to)
            )
            part["wait"].append((copy, slot[0]))
            slot[0] += piece
        part["base"], part["n"], part["phase"] = base + here * piece, piece, part["phase"] + 1
        part["path"].append((axis, part["base"], piece))

    def collect(part):
        own = pl.ds(part["base"], part["n"])
        value = acc[own]
        for copy, at in part["wait"]:
            copy.wait_recv()
            value = value + bufs[at : at + part["n"]]
        acc[own] = value

    state = []
    for copy, (base, n, order) in zip(arriving, PARTS):
        copy.wait_recv()
        acc[base : base + n] = g_ref[pl.ds(mine + base, n)] + other[base : base + n]
        part = {"base": base, "n": n, "order": order, "phase": 0, "path": []}
        state.append(part)
        scatter(part)

    @pl.when(d == depths - 1)
    def _():
        update(((0, BS),), False)

    for phase in range(3):
        for part in state:
            if phase < len(part["order"]):
                collect(part)
                if phase + 1 < len(part["order"]):
                    scatter(part)
    last = state[-1]
    own = pl.ds(last["base"], last["n"])
    ring[d] = acc[own]
    copies = []
    for off in range(1, SIZES["y"]):
        to = lax.rem(d + off, SIZES["y"])
        copies.append(start(acc.at[own], ring.at[d], device("y", to)))
    for part in state[:-1]:
        res[pl.ds(mine + part["base"], part["n"])] = acc[pl.ds(part["base"], part["n"])]

    def gather(part):
        axis, base, n = part["path"].pop()
        k, here = SIZES[axis], place[axis]
        region = res.at[pl.ds(mine + base, n)]
        part["wait"] = [start(region, region, device(axis, lax.rem(here + off, k))) for off in range(1, k)]

    for part in state[:-1]:
        gather(part)
    for copy in copies:
        copy.wait_recv()
    value = ring[0]
    for at in range(1, SIZES["y"]):
        value = value + ring[at]
    res[pl.ds(mine + last["base"], last["n"])] = value
    gather(last)

    def store(at, half, base, n):
        groups = pl.ds(half + base, n)
        copy = pltpu.make_async_copy(res.at[groups], res_hbm.at[groups], store_sem.at[at])
        copy.start()
        return copy

    finals = []
    for _ in range(3):
        for part, (base, n, _) in zip(state, PARTS):
            if part["wait"] is None:
                continue
            for copy in part["wait"]:
                copy.wait_recv()
            if part["path"]:
                gather(part)
            else:
                part["wait"] = None
                region = res.at[pl.ds(mine + base, n)]
                finals.append((start(region, region, twin), base, n))
    stores = []
    for _, base, n in finals:
        stores.append(store(len(stores), mine, base, n))
    for copy, base, n in finals:
        copy.wait_recv()
        stores.append(store(len(stores), theirs, base, n))

    for copy in stores:
        copy.wait()
    for copy in started:
        copy.wait_send()
    for p in range(len(PIECES)):
        for copy in piece_copies(p):
            copy.wait_send()
        if p < RELAYED:
            crossing(p).wait_send()

    @pl.when(d < depths - 1)
    def _():
        for at in range(count + PANELS - 1):
            handed_copy(at).wait_send()


def tile_of(i, j):
    delta = (j - i) % MB
    if delta > MB // 2 or (delta == MB // 2 and i >= MB // 2):
        return tile_of(j, i)[0], True
    if delta == MB // 2:
        return (i // 2) * HALF_TILES + 16 + i % 2, False
    return (i // 4) * HALF_TILES + delta * 4 + i % 4, False


def finish_kernel(
    u_hbm, handed_hbm, res_hbm, tip_hbm, lower_hbm, given_hbm, out_hbm,
    u, handed, res, tip, lower, out, sems, row_sems, out_sems,
):
    load_u = pltpu.make_async_copy(u_hbm, u, sems.at[0])
    load_handed = pltpu.make_async_copy(handed_hbm, handed, sems.at[1])
    load_res = [
        pltpu.make_async_copy(res_hbm.at[pl.ds(h * HALF, HALF)], res.at[pl.ds(h * HALF, HALF)], sems.at[2 + h])
        for h in range(2)
    ]
    kept = pltpu.make_async_copy(lower, lower_hbm, sems.at[4])
    given = pltpu.make_async_copy(handed, given_hbm, sems.at[5])
    row_loads, row_stores = [], []
    for i in range(MB):
        rows = pl.ds(i * BS, BS)
        row_loads.append(pltpu.make_async_copy(tip_hbm.at[rows], tip.at[rows], row_sems.at[i]))
        row_stores.append(pltpu.make_async_copy(out.at[rows], out_hbm.at[rows], out_sems.at[i]))
    for copy in [load_u, load_handed, *load_res, *row_loads]:
        copy.start()
    row = lax.broadcasted_iota(jnp.int32, (BS, BS), 0)
    col = lax.broadcasted_iota(jnp.int32, (BS, BS), 1)
    load_u.wait()
    for n in range(u.shape[0]):
        un = u[n]
        lower[n] = jnp.where(col > row, un, jnp.where(col == row, 1.0 / un, 0.0)).T
    kept.start()
    load_handed.wait()
    given.start()
    for copy in load_res:
        copy.wait()
    for i in range(MB):
        row_loads[i].wait()
        for j in range(MB):
            at, turned = tile_of(i, j)
            value = res[at * 16 : at * 16 + 16].reshape(BS, BS)
            here = (slice(i * BS, i * BS + BS), slice(j * BS, j * BS + BS))
            out[here] = tip[here] - (value.T if turned else value)
        row_stores[i].start()
    for copy in [given, kept, *row_stores]:
        copy.wait()


def body(diag_blocks, coupling, offsets, arrow_blocks, arrow_index, tip):
    count, width = offsets.shape[1:]
    spokes = arrow_index.shape[2]
    copies, room = 2 * len(PARTS) + SIZES["y"] - 1, 0
    for _, n, order in PARTS:
        for axis in order:
            n //= SIZES[axis]
            room += (SIZES[axis] - 1) * n
            copies += 2 * (SIZES[axis] - 1)
    vmem, smem, hbm = (pl.BlockSpec(memory_space=space) for space in (pltpu.VMEM, pltpu.SMEM, pl.ANY))
    blocks = jax.ShapeDtypeStruct((count, BS, BS), F32)
    band = 2 * REACH + count
    dma = pltpu.SemaphoreType.DMA
    u, handed, total = pl.pallas_call(
        kernel,
        out_shape=(blocks, blocks, jax.ShapeDtypeStruct((2 * HALF, 8, BS), F32)),
        in_specs=[hbm, hbm, smem, hbm, smem],
        out_specs=(vmem, vmem, hbm),
        scratch_shapes=[
            pltpu.VMEM((count, BS, BS), F32),
            pltpu.VMEM((count * width, BS, BS), F32),
            pltpu.VMEM((count, spokes, BS, BS), F32),
            pltpu.VMEM((count, BS, BS), F32),
            pltpu.VMEM((count, BS, BS), F32),
            pltpu.VMEM((band // 2, PANEL, BS), F32),
            pltpu.VMEM((band, PANEL, BS), F32),
            pltpu.VMEM((band, PANEL, BS), F32),
            pltpu.VMEM((band, BS, 3 * BS), BF16),
            pltpu.VMEM((count * width, 3 * BS, BS), BF16),
            pltpu.VMEM((count, 3 * BS, spokes * BS), BF16),
            pltpu.VMEM((width * BS, 2 * BS), BF16),
            pltpu.VMEM((count, BS, 2 * BS), F32),
            pltpu.VMEM((count, spokes + 1, 2, BS, BS), BF16),
            pltpu.VMEM((count * BS, 12 * BS), BF16),
            pltpu.VMEM((count * BS, 12 * BS), BF16),
            pltpu.VMEM((2 * HALF, 8, BS), F32),
            pltpu.VMEM((HALF, 8, BS), F32),
            pltpu.VMEM((HALF, 8, BS), F32),
            pltpu.VMEM((room, 8, BS), F32),
            pltpu.VMEM((SIZES["y"], 1, 8, BS), F32),
            pltpu.VMEM((2 * HALF, 8, BS), F32),
            dma((3,)),
            dma((2 * len(PARTS),)),
            dma((len(PIECES), 4)),
            dma((len(PIECES), 4)),
            dma((count + PANELS - 1,)),
            dma((count + PANELS - 1,)),
            dma((copies,)),
            dma((copies,)),
        ],
        compiler_params=pltpu.CompilerParams(
            collective_id=0, has_side_effects=True, vmem_limit_bytes=60 * 1024 * 1024
        ),
    )(diag_blocks[0], coupling[0].reshape(count * width, BS, BS), offsets[0], arrow_blocks[0], arrow_index[0])
    lower, handed, schur_tip = pl.pallas_call(
        finish_kernel,
        out_shape=(blocks, blocks, jax.ShapeDtypeStruct(tip.shape, F32)),
        in_specs=[hbm] * 4,
        out_specs=(hbm,) * 3,
        scratch_shapes=[
            pltpu.VMEM(blocks.shape, F32),
            pltpu.VMEM(blocks.shape, F32),
            pltpu.VMEM(total.shape, F32),
            pltpu.VMEM(tip.shape, F32),
            pltpu.VMEM(blocks.shape, F32),
            pltpu.VMEM(tip.shape, F32),
            dma((6,)),
            dma((MB,)),
            dma((MB,)),
        ],
        compiler_params=pltpu.CompilerParams(vmem_limit_bytes=60 * 1024 * 1024),
    )(u, handed, total, tip)
    return (lower[None], handed[None], schur_tip)


def solution(mesh):
    return jax.shard_map(
        body,
        mesh=mesh,
        in_specs=(
            P("depth", "lat", None, None),
            P("depth", "lat", None, None, None),
            P("depth", "lat", None),
            P("depth", "lat", None, None, None),
            P("depth", "lat", None),
            P(),
        ),
        out_specs=(P("depth", "lat", None, None), P("depth", "lat", None, None), P()),
        check_vma=False,
    )
```

```python
import functools

import jax
import jax.numpy as jnp
from jax import lax
from jax.experimental import pallas as pl
from jax.experimental.pallas import tpu as pltpu
from jax.sharding import PartitionSpec as P

BS = 128
PANEL = 32
PANELS = BS // PANEL
REACH = 8
MB = 8
F32 = jnp.float32
BF16 = jnp.bfloat16
MESH = pl.DeviceIdType.MESH
X, Z = 4, 8
SIZES = {"x": X, "y": 4, "z": Z}
HALF_TILES = 18
HALF = HALF_TILES * 16
PARTS = ((0, 128, "xyz"), (128, 128, "yxz"), (256, 32, "zx"))
PIECES = (
    (64, "pair", 2, 0, 32), (80, "top", 4, 0, 16), (96, "top", 4, 16, 32), (112, "all", 4, 0, 16), (128, "all", 4, 16, 32)
)
RELAYED = 3


def split2(x):
    high = x.astype(BF16)
    return high, (x - high.astype(F32)).astype(BF16)


def split3(x):
    high = x.astype(BF16)
    rest = x - high.astype(F32)
    middle = rest.astype(BF16)
    return high, middle, (rest - middle.astype(F32)).astype(BF16)


def dot(a, b):
    return jnp.dot(a, b, preferred_element_type=F32)


def dot_t(a, b):
    return lax.dot_general(a, b, (((0,), (0,)), ((), ())), preferred_element_type=F32)


def gram_exact(u, v):
    uh, um, ul = split3(u)
    vh, vm, vl = split3(v)
    return dot_t(
        jnp.concatenate([uh, uh, uh, um, um, ul], 0),
        jnp.concatenate([vh, vm, vl, vh, vm, vh], 0),
    )


def eliminate(part, j0, done):
    count = part[0].shape[0]
    shape = (count, 8, BS)
    lane = lax.broadcasted_iota(jnp.int32, shape, 2)
    sub = lax.broadcasted_iota(jnp.int32, shape, 1)
    groups = len(part)
    spread = lambda x: jnp.broadcast_to(x, shape)
    for g in range(groups):
        c0 = j0 + 8 * g
        cols = [[spread(part[v][:, :, c0 + k : c0 + k + 1]) for k in range(8)] for v in range(g, groups)]
        keep = (lane < c0) | (lane >= c0 + 8)
        x = jnp.where(keep, part[g], jnp.where(lane == c0 + sub, 1.0, 0.0))
        d = cols[0]
        scales, rows, low = [], [], {}
        for i in range(8):
            scale = lax.rsqrt(spread(d[i][:, i : i + 1, :]))
            li = d[i] * scale
            for k in range(i + 1, 8):
                low[k, i] = spread(li[:, k : k + 1, :])
                d[k] = d[k] - li * low[k, i]
            row = spread(x[:, i : i + 1, :]) * scale
            scales.append(scale)
            rows.append(row)
            x = jnp.where(sub > i, x - li * row, jnp.where(sub == i, row, x))
        for k in range(1, 8):
            for i in range(k):
                x = jnp.where((sub == i) & (lane == c0 + k), low[k, i], x)
        part[g] = x
        for v in range(g + 1, groups):
            d = cols[v - g]
            x = jnp.where(keep, part[v], 0.0)
            for i in range(8):
                mi = d[i] * scales[i]
                for k in range(i + 1, 8):
                    d[k] = d[k] - mi * low[k, i]
                x = x - mi * rows[i]
            part[v] = x
        done(g)


def kernel(
    diag_hbm, coup_hbm, off_ref, arrow_hbm, idx_ref,
    ubuf, handed_ref, res_hbm,
    dbuf, cbuf, bbuf, corr, landed, pieces, wide, cwide, bwide, stacked, placed, hi, lo,
    g_ref, other, acc, bufs, ring, res,
    load_sem, store_sem, win_send, win_recv, dep_send, dep_recv, sum_send, sum_recv,
):
    depths, lats = lax.axis_size("depth"), lax.axis_size("lat")
    d, l = lax.axis_index("depth"), lax.axis_index("lat")
    count, width = off_ref.shape
    spokes = idx_ref.shape[1]
    px, pz, c = l // (2 * Z), lax.rem(l // 2, Z), lax.rem(l, 2)
    place = {"x": px, "y": d, "z": pz}
    twin = (d, l + 1 - 2 * c)

    def device(axis, index):
        if axis == "y":
            return (index, l)
        if axis == "x":
            return (d, (index * Z + pz) * 2 + c)
        return (d, (px * Z + index) * 2 + c)

    def lat_at(step):
        return (d, lax.rem(l + step + lats, lats))

    def remote(src, dst, send, recv, peer):
        return pltpu.make_async_remote_copy(
            src_ref=src, dst_ref=dst, send_sem=send, recv_sem=recv, device_id=peer, device_id_type=MESH
        )

    loads = [
        pltpu.make_async_copy(src, dst, load_sem.at[at])
        for at, (src, dst) in enumerate(((diag_hbm, dbuf), (coup_hbm, cbuf), (arrow_hbm, bbuf)))
    ]
    loads[0].start()

    barrier = pltpu.get_barrier_semaphore()
    peers = [twin, lat_at(-2), lat_at(2), lat_at(2 * c - 1)]
    for axis in "xyz":
        peers += [device(axis, lax.rem(place[axis] + off, SIZES[axis])) for off in range(1, SIZES[axis])]
    for peer in peers:
        pl.semaphore_signal(barrier, inc=1, device_id=peer, device_id_type=MESH)

    def prepare():
        def couple(at, _):
            ch, cl = split2(cbuf[at])
            cwide[at] = jnp.concatenate(
                [jnp.concatenate([ch, cl], 1), jnp.concatenate([ch, jnp.zeros_like(ch)], 1)], 0
            )
            return 0

        def spoke(n, _):
            for s in range(spokes):
                bh, bl = split2(bbuf[n, s])
                bwide[n, :, s * BS : (s + 1) * BS] = jnp.concatenate([bh, bh, bl], 0)
            placed[n, spokes] = jnp.zeros(placed.shape[2:], BF16)
            return 0

        loads[1].wait()
        loads[2].wait()
        lax.fori_loop(0, count * width, couple, 0)
        lax.fori_loop(0, count, spoke, 0)

    def handed_copy(at):
        if at < count:
            rows = (at, pl.ds(0, PANEL))
        else:
            rows = (slice(None), pl.ds((at - count + 1) * PANEL, PANEL))
        return remote(
            handed_ref.at[rows], landed.at[rows], dep_send.at[at], dep_recv.at[at],
            (lax.rem(d + 1, depths), l),
        )

    @pl.when(d == 0)
    def _():
        landed[...] = jnp.zeros_like(landed)

    loads[0].wait()
    loads[1].start()
    loads[2].start()

    @pl.when(d > 0)
    def _():
        prepare()

    def place_of(step, p):
        blocks = PIECES[p][2]
        return pieces[p].at[pl.ds(step * blocks, blocks)]

    def received(p, at, step):
        return remote(place_of(2, p), place_of(step, p), win_send.at[p, at], win_recv.at[p, at], twin)

    def piece_copies(p):
        own = place_of(2, p)
        copies = [
            remote(own, place_of(4, p), win_send.at[p, 0], win_recv.at[p, 0], lat_at(-2)),
            remote(own, place_of(0, p), win_send.at[p, 1], win_recv.at[p, 1], lat_at(2)),
            remote(own, place_of(1 + 2 * c, p), win_send.at[p, 2], win_recv.at[p, 2], twin),
        ]
        if p >= RELAYED:
            copies.append(crossing(p))
        return copies

    def crossing(p):
        if p < RELAYED:
            src, peer = place_of(4 - 4 * c, p), twin
        else:
            src, peer = place_of(2, p), lat_at(2 * c - 1)
        return remote(src, place_of(3 - 2 * c, p), win_send.at[p, 3], win_recv.at[p, 3], peer)

    def hand_over(p):
        received(p, c, 4 - 4 * c).wait_recv()
        if p < RELAYED:
            crossing(p).start()

    def wait_piece(p):
        received(p, 1 - c, 4 * c).wait_recv()
        received(p, 2, 1 + 2 * c).wait_recv()
        crossing(p).wait_recv()

    def pack(p):
        end, kind, blocks, first, last = PIECES[p]
        rows = end - (last - first)
        value = ubuf[:, rows:end, :]
        lane = lax.broadcasted_iota(jnp.int32, value.shape, 2)
        value = jnp.where(lane <= rows + lax.broadcasted_iota(jnp.int32, value.shape, 1), value, 0.0)
        if kind == "pair":
            half = lane[:2] < BS // 2
            value = jnp.where(half, value[:2], pltpu.roll(value[2:], BS // 2, 2))
        elif kind == "top":
            top = ubuf[:, first:last, :]
            top = jnp.where(lane <= first + lax.broadcasted_iota(jnp.int32, top.shape, 1), top, 0.0)
            value = jnp.where(lane < BS - PANEL, value, pltpu.roll(top, BS - PANEL, 2))
        pieces[p][2 * blocks : 3 * blocks] = value

    def widen(rows, blocks, value):
        high, low = split2(value)
        wide[blocks, rows, :] = jnp.concatenate([high, low], 2)

    def unpack(which):
        for step in range(5):
            inside = (l + step >= 2) & (l + step < lats + 2)
            at = step * count
            for p in which:
                end, kind, blocks, first, last = PIECES[p]
                rows = slice(end - (last - first), end)
                value = jnp.where(inside, pieces[p][step * blocks : (step + 1) * blocks], 0.0)
                lane = lax.broadcasted_iota(jnp.int32, value.shape, 2)
                if kind == "pair":
                    half = lane < BS // 2
                    widen(rows, slice(at, at + 2), jnp.where(half, value, 0.0))
                    widen(rows, slice(at + 2, at + 4), jnp.where(half, pltpu.roll(value, BS // 2, 2), 0.0))
                elif kind == "top":
                    widen(rows, slice(at, at + count), jnp.where(lane < BS - PANEL, value, 0.0))
                    top = jnp.where(lane < PANEL, pltpu.roll(value, PANEL, 2), 0.0)
                    widen(slice(first, last), slice(at, at + count), top)
                else:
                    widen(rows, slice(at, at + count), value)

    for p in range(PANELS):
        j0, end = p * PANEL, (p + 1) * PANEL
        needed = (count + p - 1,) if p else range(count)

        @pl.when(d > 0)
        def _():
            for at in needed:
                handed_copy(at).wait_recv()

        a = dbuf[:, j0:end, :] + landed[:, j0:end, :]
        lane = lax.broadcasted_iota(jnp.int32, a.shape, 2)
        row = j0 + lax.broadcasted_iota(jnp.int32, a.shape, 1)
        if p:
            a = jnp.where(lane < j0, 0.0, a) - corr[:, j0:end, :]
        part = [a[:, 8 * v : 8 * v + 8] for v in range(PANEL // 8)]

        def done(g):
            if g % 2 == 0:
                return
            row = j0 + 8 * g - 8
            ubuf[:, row : row + 16, :] = jnp.concatenate(part[g - 1 : g + 1], 1)
            for at, piece in enumerate(PIECES):
                if piece[0] == row + 16:
                    pack(at)
                    if at == 0:
                        pl.semaphore_wait(barrier, len(peers))
                    for copy in piece_copies(at):
                        copy.start()
            if row + 16 == PIECES[3][0]:
                hand_over(0)

        eliminate(part, j0, done)
        if end < BS:
            u = jnp.concatenate(part, 1)
            right = jnp.where((lane < end) & (lane > row), 0.0, u)
            for m in range(count):
                full = gram_exact(u[m], right[m])[end:]
                if p:
                    old = corr[m, end:, :]
                    ln = lax.broadcasted_iota(jnp.int32, old.shape, 1)
                    full = full + jnp.where((ln >= j0) & (ln < end), 0.0, old)
                corr[m, end:, :] = full

    def update(hand_on):
        for p in range(1, RELAYED):
            hand_over(p)

        @pl.when(d == 0)
        def _():
            prepare()

        for p in range(RELAYED):
            wait_piece(p)
        unpack(range(RELAYED))
        for p in range(RELAYED, len(PIECES)):
            hand_over(p)
            wait_piece(p)
        unpack(range(RELAYED, len(PIECES)))
        for m in range(count):
            for w in range(width):
                x = dot(wide[off_ref[m, w] + (m + REACH)], cwide[m * width + w])
                xh, xl = split2(x[:, :BS] + x[:, BS:])
                stacked[m, w * BS : (w + 1) * BS, :] = jnp.concatenate([xh, xl], 1)
        for m in range(count):
            both = dot_t(stacked[m, :, :BS], stacked[m])
            cross = both[:, BS:]
            handed_ref[m] = -(both[:, :BS] + cross + cross.T)
            if hand_on:
                handed_copy(m).start()
        if hand_on:
            for p in range(1, PANELS):
                handed_copy(count + p - 1).start()

    @pl.when(d < depths - 1)
    def _():
        update(True)

    row = lax.broadcasted_iota(jnp.int32, (BS, BS), 0)
    col = lax.broadcasted_iota(jnp.int32, (BS, BS), 1)
    for n in range(count):
        high, low = split2(jnp.where(col <= row, ubuf[n], 0.0))
        t = dot(jnp.concatenate([high, low, high], 1), bwide[n])
        for s in range(spokes):
            th, tl = split2(t[:, s * BS : (s + 1) * BS])
            placed[n, s, 0] = th
            placed[n, s, 1] = tl
    for n in range(count):
        for m in range(MB):
            slot = spokes
            for s in range(spokes):
                slot = jnp.where(idx_ref[n, s] == m, s, slot)
            both = placed[n, slot]
            for at in (m, m + MB)[: 2 if m < MB // 2 else 1]:
                hi[n * BS : (n + 1) * BS, at * BS : (at + 1) * BS] = both[0]
                lo[n * BS : (n + 1) * BS, at * BS : (at + 1) * BS] = both[1]

    def tile_product(i, first, tiles):
        left = pl.ds(pl.multiple_of(i * BS, BS), BS)
        right = pl.ds(pl.multiple_of(first * BS, BS), tiles * BS)
        return dot_t(hi[:, left], hi[:, right]) + dot_t(hi[:, left], lo[:, right]) + dot_t(lo[:, left], hi[:, right])

    def put(h, k, value):
        g_ref[pl.ds((h * HALF_TILES + k) * 16, 16)] = value.reshape(16, 8, BS)

    def half_products(h):
        for ii in range(4):
            product = tile_product(4 * h + ii, 4 * h + ii, 4)
            for delta in range(4):
                put(h, delta * 4 + ii, product[:, delta * BS : (delta + 1) * BS])
        for ii in range(2):
            put(h, 16 + ii, tile_product(2 * h + ii, 2 * h + ii + 4, 1))

    used = [0]
    started = []

    def start(src, dst, peer):
        at = used[0]
        used[0] += 1
        copy = remote(src, dst, sum_send.at[at], sum_recv.at[at], peer)
        copy.start()
        started.append(copy)
        return copy

    mine, theirs = c * HALF, (1 - c) * HALF
    half_products(1 - c)
    arriving = [start(g_ref.at[pl.ds(theirs + at, n)], other.at[pl.ds(at, n)], twin) for at, n, _ in PARTS]
    half_products(c)
    slot = [0]

    def scatter(part):
        axis = part["order"][part["phase"]]
        k, here = SIZES[axis], place[axis]
        base, piece = part["base"], part["n"] // k
        part["wait"] = []
        for off in range(1, k):
            to = lax.rem(here + off, k)
            copy = start(
                acc.at[pl.ds(base + to * piece, piece)], bufs.at[pl.ds(slot[0], piece)], device(axis, to)
            )
            part["wait"].append((copy, slot[0]))
            slot[0] += piece
        part["base"], part["n"], part["phase"] = base + here * piece, piece, part["phase"] + 1
        part["path"].append((axis, part["base"], piece))

    def collect(part):
        own = pl.ds(part["base"], part["n"])
        value = acc[own]
        for copy, at in part["wait"]:
            copy.wait_recv()
            value = value + bufs[at : at + part["n"]]
        acc[own] = value

    state = []
    for copy, (base, n, order) in zip(arriving, PARTS):
        copy.wait_recv()
        acc[base : base + n] = g_ref[pl.ds(mine + base, n)] + other[base : base + n]
        part = {"base": base, "n": n, "order": order, "phase": 0, "path": []}
        state.append(part)
        scatter(part)

    @pl.when(d == depths - 1)
    def _():
        update(False)

    for phase in range(3):
        for part in state:
            if phase < len(part["order"]):
                collect(part)
                if phase + 1 < len(part["order"]):
                    scatter(part)
    last = state[-1]
    own = pl.ds(last["base"], last["n"])
    ring[d] = acc[own]
    copies = []
    for off in range(1, SIZES["y"]):
        to = lax.rem(d + off, SIZES["y"])
        copies.append(start(acc.at[own], ring.at[d], device("y", to)))
    for part in state[:-1]:
        res[pl.ds(mine + part["base"], part["n"])] = acc[pl.ds(part["base"], part["n"])]

    def gather(part):
        axis, base, n = part["path"].pop()
        k, here = SIZES[axis], place[axis]
        region = res.at[pl.ds(mine + base, n)]
        part["wait"] = [start(region, region, device(axis, lax.rem(here + off, k))) for off in range(1, k)]

    for part in state[:-1]:
        gather(part)
    for copy in copies:
        copy.wait_recv()
    value = ring[0]
    for at in range(1, SIZES["y"]):
        value = value + ring[at]
    res[pl.ds(mine + last["base"], last["n"])] = value
    gather(last)

    def store(at, half, base, n):
        groups = pl.ds(half + base, n)
        copy = pltpu.make_async_copy(res.at[groups], res_hbm.at[groups], store_sem.at[at])
        copy.start()
        return copy

    finals = []
    for _ in range(3):
        for part, (base, n, _) in zip(state, PARTS):
            if part["wait"] is None:
                continue
            for copy in part["wait"]:
                copy.wait_recv()
            if part["path"]:
                gather(part)
            else:
                part["wait"] = None
                region = res.at[pl.ds(mine + base, n)]
                finals.append((start(region, region, twin), base, n))
    stores = []
    for _, base, n in finals:
        stores.append(store(len(stores), mine, base, n))
    for copy, base, n in finals:
        copy.wait_recv()
        stores.append(store(len(stores), theirs, base, n))

    for copy in stores:
        copy.wait()
    for copy in started:
        copy.wait_send()
    for p in range(len(PIECES)):
        for copy in piece_copies(p):
            copy.wait_send()
        if p < RELAYED:
            crossing(p).wait_send()

    @pl.when(d < depths - 1)
    def _():
        for at in range(count + PANELS - 1):
            handed_copy(at).wait_send()


def tile_of(i, j):
    delta = (j - i) % MB
    if delta > MB // 2 or (delta == MB // 2 and i >= MB // 2):
        return tile_of(j, i)[0], True
    if delta == MB // 2:
        return (i // 2) * HALF_TILES + 16 + i % 2, False
    return (i // 4) * HALF_TILES + delta * 4 + i % 4, False


def finish_kernel(
    u_hbm, handed_hbm, res_hbm, tip_hbm, lower_hbm, given_hbm, out_hbm,
    u, handed, res, tip, lower, out, sems, row_sems, out_sems,
):
    load_u = pltpu.make_async_copy(u_hbm, u, sems.at[0])
    load_handed = pltpu.make_async_copy(handed_hbm, handed, sems.at[1])
    load_res = [
        pltpu.make_async_copy(res_hbm.at[pl.ds(h * HALF, HALF)], res.at[pl.ds(h * HALF, HALF)], sems.at[2 + h])
        for h in range(2)
    ]
    kept = pltpu.make_async_copy(lower, lower_hbm, sems.at[4])
    given = pltpu.make_async_copy(handed, given_hbm, sems.at[5])
    row_loads, row_stores = [], []
    for i in range(MB):
        rows = pl.ds(i * BS, BS)
        row_loads.append(pltpu.make_async_copy(tip_hbm.at[rows], tip.at[rows], row_sems.at[i]))
        row_stores.append(pltpu.make_async_copy(out.at[rows], out_hbm.at[rows], out_sems.at[i]))
    for copy in [load_u, load_handed, *load_res, *row_loads]:
        copy.start()
    row = lax.broadcasted_iota(jnp.int32, (BS, BS), 0)
    col = lax.broadcasted_iota(jnp.int32, (BS, BS), 1)
    load_u.wait()
    for n in range(u.shape[0]):
        un = u[n]
        lower[n] = jnp.where(col > row, un, jnp.where(col == row, 1.0 / un, 0.0)).T
    kept.start()
    load_handed.wait()
    given.start()
    for copy in load_res:
        copy.wait()
    for i in range(MB):
        row_loads[i].wait()
        for j in range(MB):
            at, turned = tile_of(i, j)
            value = res[at * 16 : at * 16 + 16].reshape(BS, BS)
            here = (slice(i * BS, i * BS + BS), slice(j * BS, j * BS + BS))
            out[here] = tip[here] - (value.T if turned else value)
        row_stores[i].start()
    for copy in [given, kept, *row_stores]:
        copy.wait()


def body(diag_blocks, coupling, offsets, arrow_blocks, arrow_index, tip):
    count, width = offsets.shape[1:]
    spokes = arrow_index.shape[2]
    copies, room = 2 * len(PARTS) + SIZES["y"] - 1, 0
    for _, n, order in PARTS:
        for axis in order:
            n //= SIZES[axis]
            room += (SIZES[axis] - 1) * n
            copies += 2 * (SIZES[axis] - 1)
    vmem, smem, hbm = (pl.BlockSpec(memory_space=space) for space in (pltpu.VMEM, pltpu.SMEM, pl.ANY))
    blocks = jax.ShapeDtypeStruct((count, BS, BS), F32)
    band = 2 * REACH + count
    dma = pltpu.SemaphoreType.DMA
    u, handed, total = pl.pallas_call(
        kernel,
        out_shape=(blocks, blocks, jax.ShapeDtypeStruct((2 * HALF, 8, BS), F32)),
        in_specs=[hbm, hbm, smem, hbm, smem],
        out_specs=(vmem, vmem, hbm),
        scratch_shapes=[
            pltpu.VMEM((count, BS, BS), F32),
            pltpu.VMEM((count * width, BS, BS), F32),
            pltpu.VMEM((count, spokes, BS, BS), F32),
            pltpu.VMEM((count, BS, BS), F32),
            pltpu.VMEM((count, BS, BS), F32),
            tuple(pltpu.VMEM((5 * blocks, last - first, BS), F32) for _, _, blocks, first, last in PIECES),
            pltpu.VMEM((band, BS, 2 * BS), BF16),
            pltpu.VMEM((count * width, 2 * BS, 2 * BS), BF16),
            pltpu.VMEM((count, 3 * BS, spokes * BS), BF16),
            pltpu.VMEM((count, width * BS, 2 * BS), BF16),
            pltpu.VMEM((count, spokes + 1, 2, BS, BS), BF16),
            pltpu.VMEM((count * BS, 12 * BS), BF16),
            pltpu.VMEM((count * BS, 12 * BS), BF16),
            pltpu.VMEM((2 * HALF, 8, BS), F32),
            pltpu.VMEM((HALF, 8, BS), F32),
            pltpu.VMEM((HALF, 8, BS), F32),
            pltpu.VMEM((room, 8, BS), F32),
            pltpu.VMEM((SIZES["y"], 1, 8, BS), F32),
            pltpu.VMEM((2 * HALF, 8, BS), F32),
            dma((3,)),
            dma((2 * len(PARTS),)),
            dma((len(PIECES), 4)),
            dma((len(PIECES), 4)),
            dma((count + PANELS - 1,)),
            dma((count + PANELS - 1,)),
            dma((copies,)),
            dma((copies,)),
        ],
        compiler_params=pltpu.CompilerParams(
            collective_id=0, has_side_effects=True, vmem_limit_bytes=60 * 1024 * 1024
        ),
    )(diag_blocks[0], coupling[0].reshape(count * width, BS, BS), offsets[0], arrow_blocks[0], arrow_index[0])
    lower, handed, schur_tip = pl.pallas_call(
        finish_kernel,
        out_shape=(blocks, blocks, jax.ShapeDtypeStruct(tip.shape, F32)),
        in_specs=[hbm] * 4,
        out_specs=(hbm,) * 3,
        scratch_shapes=[
            pltpu.VMEM(blocks.shape, F32),
            pltpu.VMEM(blocks.shape, F32),
            pltpu.VMEM(total.shape, F32),
            pltpu.VMEM(tip.shape, F32),
            pltpu.VMEM(blocks.shape, F32),
            pltpu.VMEM(tip.shape, F32),
            dma((6,)),
            dma((MB,)),
            dma((MB,)),
        ],
        compiler_params=pltpu.CompilerParams(vmem_limit_bytes=60 * 1024 * 1024),
    )(u, handed, total, tip)
    return (lower[None], handed[None], schur_tip)


def solution(mesh):
    return jax.shard_map(
        body,
        mesh=mesh,
        in_specs=(
            P("depth", "lat", None, None),
            P("depth", "lat", None, None, None),
            P("depth", "lat", None),
            P("depth", "lat", None, None, None),
            P("depth", "lat", None),
            P(),
        ),
        out_specs=(P("depth", "lat", None, None), P("depth", "lat", None, None), P()),
        check_vma=False,
    )
```

```python
import functools

import jax
import jax.numpy as jnp
from jax import lax
from jax.experimental import pallas as pl
from jax.experimental.pallas import tpu as pltpu
from jax.sharding import PartitionSpec as P

BS = 128
PANEL = 32
PANELS = BS // PANEL
REACH = 8
MB = 8
F32 = jnp.float32
BF16 = jnp.bfloat16
MESH = pl.DeviceIdType.MESH
X, Z = 4, 8
SIZES = {"x": X, "y": 4, "z": Z}
HALF_TILES = 18
HALF = HALF_TILES * 16
PARTS = ((0, 128, "xyz"), (128, 128, "yxz"), (256, 32, "zx"))
PIECES = (
    (64, "pair", 2, 0, 32), (80, "top", 4, 0, 16), (96, "top", 4, 16, 32), (112, "all", 4, 0, 16), (128, "all", 4, 16, 32)
)
RELAYED = 4


def split2(x):
    high = x.astype(BF16)
    return high, (x - high.astype(F32)).astype(BF16)


def split3(x):
    high = x.astype(BF16)
    rest = x - high.astype(F32)
    middle = rest.astype(BF16)
    return high, middle, (rest - middle.astype(F32)).astype(BF16)


def dot(a, b):
    return jnp.dot(a, b, preferred_element_type=F32)


def dot_t(a, b):
    return lax.dot_general(a, b, (((0,), (0,)), ((), ())), preferred_element_type=F32)


def gram_exact(u, v):
    uh, um, ul = split3(u)
    vh, vm, vl = split3(v)
    return dot_t(
        jnp.concatenate([uh, uh, uh, um, um, ul], 0),
        jnp.concatenate([vh, vm, vl, vh, vm, vh], 0),
    )


def eliminate(part, j0, done):
    count = part[0].shape[0]
    shape = (count, 8, BS)
    lane = lax.broadcasted_iota(jnp.int32, shape, 2)
    sub = lax.broadcasted_iota(jnp.int32, shape, 1)
    groups = len(part)
    spread = lambda x: jnp.broadcast_to(x, shape)
    for g in range(groups):
        c0 = j0 + 8 * g
        cols = [[spread(part[v][:, :, c0 + k : c0 + k + 1]) for k in range(8)] for v in range(g, groups)]
        keep = (lane < c0) | (lane >= c0 + 8)
        x = jnp.where(keep, part[g], jnp.where(lane == c0 + sub, 1.0, 0.0))
        d = cols[0]
        scales, rows, low = [], [], {}
        for i in range(8):
            scale = lax.rsqrt(spread(d[i][:, i : i + 1, :]))
            li = d[i] * scale
            for k in range(i + 1, 8):
                low[k, i] = spread(li[:, k : k + 1, :])
                d[k] = d[k] - li * low[k, i]
            row = spread(x[:, i : i + 1, :]) * scale
            scales.append(scale)
            rows.append(row)
            x = jnp.where(sub > i, x - li * row, jnp.where(sub == i, row, x))
        for k in range(1, 8):
            for i in range(k):
                x = jnp.where((sub == i) & (lane == c0 + k), low[k, i], x)
        part[g] = x
        for v in range(g + 1, groups):
            d = cols[v - g]
            x = jnp.where(keep, part[v], 0.0)
            for i in range(8):
                mi = d[i] * scales[i]
                for k in range(i + 1, 8):
                    d[k] = d[k] - mi * low[k, i]
                x = x - mi * rows[i]
            part[v] = x
        done(g)


def kernel(
    diag_hbm, coup_hbm, off_ref, arrow_hbm, idx_ref,
    u_hbm, handed_hbm, res_hbm,
    ubuf, handed_ref, dbuf, cbuf, bbuf, corr, landed, pieces, wide, cwide, bwide, stacked, placed, hi, lo,
    g_ref, other, acc, bufs, ring, res,
    load_sem, store_sem, keep_sem, win_send, win_recv, dep_send, dep_recv, sum_send, sum_recv,
):
    depths, lats = lax.axis_size("depth"), lax.axis_size("lat")
    d, l = lax.axis_index("depth"), lax.axis_index("lat")
    count, width = off_ref.shape
    spokes = idx_ref.shape[1]
    px, pz, c = l // (2 * Z), lax.rem(l // 2, Z), lax.rem(l, 2)
    place = {"x": px, "y": d, "z": pz}
    twin = (d, l + 1 - 2 * c)

    def device(axis, index):
        if axis == "y":
            return (index, l)
        if axis == "x":
            return (d, (index * Z + pz) * 2 + c)
        return (d, (px * Z + index) * 2 + c)

    def lat_at(step):
        return (d, lax.rem(l + step + lats, lats))

    def remote(src, dst, send, recv, peer):
        return pltpu.make_async_remote_copy(
            src_ref=src, dst_ref=dst, send_sem=send, recv_sem=recv, device_id=peer, device_id_type=MESH
        )

    loads = [
        pltpu.make_async_copy(src, dst, load_sem.at[at])
        for at, (src, dst) in enumerate(((diag_hbm, dbuf), (coup_hbm, cbuf), (arrow_hbm, bbuf)))
    ]
    loads[0].start()

    keep_u = pltpu.make_async_copy(ubuf, u_hbm, keep_sem.at[0])
    keep_handed = pltpu.make_async_copy(handed_ref, handed_hbm, keep_sem.at[1])

    barrier = pltpu.get_barrier_semaphore()
    peers = [twin, lat_at(-2), lat_at(2), lat_at(2 * c - 1)]
    for axis in "xyz":
        peers += [device(axis, lax.rem(place[axis] + off, SIZES[axis])) for off in range(1, SIZES[axis])]
    for peer in peers:
        pl.semaphore_signal(barrier, inc=1, device_id=peer, device_id_type=MESH)

    def prepare():
        def couple(at, _):
            ch, cl = split2(cbuf[at])
            cwide[at] = jnp.concatenate(
                [jnp.concatenate([ch, cl], 1), jnp.concatenate([ch, jnp.zeros_like(ch)], 1)], 0
            )
            return 0

        def spoke(n, _):
            for s in range(spokes):
                bh, bl = split2(bbuf[n, s])
                bwide[n, :, s * BS : (s + 1) * BS] = jnp.concatenate([bh, bh, bl], 0)
            placed[n, spokes] = jnp.zeros(placed.shape[2:], BF16)
            return 0

        loads[1].wait()
        loads[2].wait()
        lax.fori_loop(0, count * width, couple, 0)
        lax.fori_loop(0, count, spoke, 0)

    def handed_copy(at):
        if at < count:
            rows = (at, pl.ds(0, PANEL))
        else:
            rows = (slice(None), pl.ds((at - count + 1) * PANEL, PANEL))
        return remote(
            handed_ref.at[rows], landed.at[rows], dep_send.at[at], dep_recv.at[at],
            (lax.rem(d + 1, depths), l),
        )

    @pl.when(d == 0)
    def _():
        landed[...] = jnp.zeros_like(landed)

    loads[0].wait()
    loads[1].start()
    loads[2].start()

    @pl.when(d > 0)
    def _():
        prepare()

    def place_of(step, p):
        blocks = PIECES[p][2]
        return pieces[p].at[pl.ds(step * blocks, blocks)]

    def received(p, at, step):
        return remote(place_of(2, p), place_of(step, p), win_send.at[p, at], win_recv.at[p, at], twin)

    def piece_copies(p):
        own = place_of(2, p)
        copies = [
            remote(own, place_of(4, p), win_send.at[p, 0], win_recv.at[p, 0], lat_at(-2)),
            remote(own, place_of(0, p), win_send.at[p, 1], win_recv.at[p, 1], lat_at(2)),
            remote(own, place_of(1 + 2 * c, p), win_send.at[p, 2], win_recv.at[p, 2], twin),
        ]
        if p >= RELAYED:
            copies.append(crossing(p))
        return copies

    def crossing(p):
        if p < RELAYED:
            src, peer = place_of(4 - 4 * c, p), twin
        else:
            src, peer = place_of(2, p), lat_at(2 * c - 1)
        return remote(src, place_of(3 - 2 * c, p), win_send.at[p, 3], win_recv.at[p, 3], peer)

    def hand_over(p):
        received(p, c, 4 - 4 * c).wait_recv()
        if p < RELAYED:
            crossing(p).start()

    def wait_piece(p):
        received(p, 1 - c, 4 * c).wait_recv()
        received(p, 2, 1 + 2 * c).wait_recv()
        crossing(p).wait_recv()

    def pack(p):
        end, kind, blocks, first, last = PIECES[p]
        rows = end - (last - first)
        value = ubuf[:, rows:end, :]
        lane = lax.broadcasted_iota(jnp.int32, value.shape, 2)
        value = jnp.where(lane <= rows + lax.broadcasted_iota(jnp.int32, value.shape, 1), value, 0.0)
        if kind == "pair":
            half = lane[:2] < BS // 2
            value = jnp.where(half, value[:2], pltpu.roll(value[2:], BS // 2, 2))
        elif kind == "top":
            top = ubuf[:, first:last, :]
            top = jnp.where(lane <= first + lax.broadcasted_iota(jnp.int32, top.shape, 1), top, 0.0)
            value = jnp.where(lane < BS - PANEL, value, pltpu.roll(top, BS - PANEL, 2))
        pieces[p][2 * blocks : 3 * blocks] = value

    def widen(rows, blocks, value):
        high, low = split2(value)
        wide[blocks, rows, :] = jnp.concatenate([high, low], 2)

    def unpack(which):
        for step in range(5):
            inside = (l + step >= 2) & (l + step < lats + 2)
            at = step * count
            for p in which:
                end, kind, blocks, first, last = PIECES[p]
                rows = slice(end - (last - first), end)
                value = jnp.where(inside, pieces[p][step * blocks : (step + 1) * blocks], 0.0)
                lane = lax.broadcasted_iota(jnp.int32, value.shape, 2)
                if kind == "pair":
                    half = lane < BS // 2
                    widen(rows, slice(at, at + 2), jnp.where(half, value, 0.0))
                    widen(rows, slice(at + 2, at + 4), jnp.where(half, pltpu.roll(value, BS // 2, 2), 0.0))
                elif kind == "top":
                    widen(rows, slice(at, at + count), jnp.where(lane < BS - PANEL, value, 0.0))
                    top = jnp.where(lane < PANEL, pltpu.roll(value, PANEL, 2), 0.0)
                    widen(slice(first, last), slice(at, at + count), top)
                else:
                    widen(rows, slice(at, at + count), value)

    for p in range(PANELS):
        j0, end = p * PANEL, (p + 1) * PANEL
        needed = (count + p - 1,) if p else range(count)

        @pl.when(d > 0)
        def _():
            for at in needed:
                handed_copy(at).wait_recv()

        a = dbuf[:, j0:end, :] + landed[:, j0:end, :]
        lane = lax.broadcasted_iota(jnp.int32, a.shape, 2)
        row = j0 + lax.broadcasted_iota(jnp.int32, a.shape, 1)
        if p:
            a = jnp.where(lane < j0, 0.0, a) - corr[:, j0:end, :]
        part = [a[:, 8 * v : 8 * v + 8] for v in range(PANEL // 8)]

        def done(g):
            if g % 2 == 0:
                return
            row = j0 + 8 * g - 8
            ubuf[:, row : row + 16, :] = jnp.concatenate(part[g - 1 : g + 1], 1)
            for at, piece in enumerate(PIECES):
                if piece[0] == row + 16:
                    pack(at)
                    if at == 0:
                        pl.semaphore_wait(barrier, len(peers))
                    for copy in piece_copies(at):
                        copy.start()
            if row + 16 == 112:
                hand_over(0)

        eliminate(part, j0, done)
        if end < BS:
            u = jnp.concatenate(part, 1)
            right = jnp.where((lane < end) & (lane > row), 0.0, u)
            for m in range(count):
                full = gram_exact(u[m], right[m])[end:]
                if p:
                    old = corr[m, end:, :]
                    ln = lax.broadcasted_iota(jnp.int32, old.shape, 1)
                    full = full + jnp.where((ln >= j0) & (ln < end), 0.0, old)
                corr[m, end:, :] = full

    def update(hand_on):
        for p in range(1, RELAYED):
            hand_over(p)

        @pl.when(d == 0)
        def _():
            prepare()

        for p in range(RELAYED):
            wait_piece(p)
        unpack(range(RELAYED))
        for p in range(RELAYED, len(PIECES)):
            hand_over(p)
            wait_piece(p)
        unpack(range(RELAYED, len(PIECES)))
        for m in range(count):
            for w in range(width):
                x = dot(wide[off_ref[m, w] + (m + REACH)], cwide[m * width + w])
                xh, xl = split2(x[:, :BS] + x[:, BS:])
                stacked[m, w * BS : (w + 1) * BS, :] = jnp.concatenate([xh, xl], 1)
        for m in range(count):
            both = dot_t(stacked[m, :, :BS], stacked[m])
            cross = both[:, BS:]
            handed_ref[m] = -(both[:, :BS] + cross + cross.T)
            if hand_on:
                handed_copy(m).start()
        if hand_on:
            for p in range(1, PANELS):
                handed_copy(count + p - 1).start()
        keep_handed.start()

    keep_u.start()

    @pl.when(d < depths - 1)
    def _():
        update(True)

    row = lax.broadcasted_iota(jnp.int32, (BS, BS), 0)
    col = lax.broadcasted_iota(jnp.int32, (BS, BS), 1)
    for n in range(count):
        high, low = split2(jnp.where(col <= row, ubuf[n], 0.0))
        t = dot(jnp.concatenate([high, low, high], 1), bwide[n])
        for s in range(spokes):
            th, tl = split2(t[:, s * BS : (s + 1) * BS])
            placed[n, s, 0] = th
            placed[n, s, 1] = tl
    for n in range(count):
        for m in range(MB):
            slot = spokes
            for s in range(spokes):
                slot = jnp.where(idx_ref[n, s] == m, s, slot)
            both = placed[n, slot]
            for at in (m, m + MB)[: 2 if m < MB // 2 else 1]:
                hi[n * BS : (n + 1) * BS, at * BS : (at + 1) * BS] = both[0]
                lo[n * BS : (n + 1) * BS, at * BS : (at + 1) * BS] = both[1]

    def tile_product(i, first, tiles):
        left = pl.ds(pl.multiple_of(i * BS, BS), BS)
        right = pl.ds(pl.multiple_of(first * BS, BS), tiles * BS)
        high, n = hi[:, right], tiles * BS
        both = dot_t(hi[:, left], jnp.concatenate([high, lo[:, right]], 1))
        return both[:, :n] + both[:, n:] + dot_t(lo[:, left], high)

    def put(h, k, value):
        g_ref[pl.ds((h * HALF_TILES + k) * 16, 16)] = value.reshape(16, 8, BS)

    def half_products(h):
        for ii in range(4):
            product = tile_product(4 * h + ii, 4 * h + ii, 4)
            for delta in range(4):
                put(h, delta * 4 + ii, product[:, delta * BS : (delta + 1) * BS])
        for ii in range(2):
            put(h, 16 + ii, tile_product(2 * h + ii, 2 * h + ii + 4, 1))

    used = [0]
    started = []

    def start(src, dst, peer):
        at = used[0]
        used[0] += 1
        copy = remote(src, dst, sum_send.at[at], sum_recv.at[at], peer)
        copy.start()
        started.append(copy)
        return copy

    mine, theirs = c * HALF, (1 - c) * HALF
    half_products(1 - c)
    arriving = [start(g_ref.at[pl.ds(theirs + at, n)], other.at[pl.ds(at, n)], twin) for at, n, _ in PARTS]
    half_products(c)
    slot = [0]

    def scatter(part):
        axis = part["order"][part["phase"]]
        k, here = SIZES[axis], place[axis]
        base, piece = part["base"], part["n"] // k
        part["wait"] = []
        for off in range(1, k):
            to = lax.rem(here + off, k)
            copy = start(
                acc.at[pl.ds(base + to * piece, piece)], bufs.at[pl.ds(slot[0], piece)], device(axis, to)
            )
            part["wait"].append((copy, slot[0]))
            slot[0] += piece
        part["base"], part["n"], part["phase"] = base + here * piece, piece, part["phase"] + 1
        part["path"].append((axis, part["base"], piece))

    def collect(part):
        own = pl.ds(part["base"], part["n"])
        value = acc[own]
        for copy, at in part["wait"]:
            copy.wait_recv()
            value = value + bufs[at : at + part["n"]]
        acc[own] = value

    state = []
    for copy, (base, n, order) in zip(arriving, PARTS):
        copy.wait_recv()
        acc[base : base + n] = g_ref[pl.ds(mine + base, n)] + other[base : base + n]
        part = {"base": base, "n": n, "order": order, "phase": 0, "path": []}
        state.append(part)
        scatter(part)

    @pl.when(d == depths - 1)
    def _():
        update(False)

    for phase in range(3):
        for part in state:
            if phase < len(part["order"]):
                collect(part)
                if phase + 1 < len(part["order"]):
                    scatter(part)
    last = state[-1]
    own = pl.ds(last["base"], last["n"])
    ring[d] = acc[own]
    copies = []
    for off in range(1, SIZES["y"]):
        to = lax.rem(d + off, SIZES["y"])
        copies.append(start(acc.at[own], ring.at[d], device("y", to)))
    for part in state[:-1]:
        res[pl.ds(mine + part["base"], part["n"])] = acc[pl.ds(part["base"], part["n"])]

    def gather(part):
        axis, base, n = part["path"].pop()
        k, here = SIZES[axis], place[axis]
        region = res.at[pl.ds(mine + base, n)]
        part["wait"] = [start(region, region, device(axis, lax.rem(here + off, k))) for off in range(1, k)]

    for part in state[:-1]:
        gather(part)
    for copy in copies:
        copy.wait_recv()
    value = ring[0]
    for at in range(1, SIZES["y"]):
        value = value + ring[at]
    res[pl.ds(mine + last["base"], last["n"])] = value
    gather(last)

    def store(at, half, base, n):
        groups = pl.ds(half + base, n)
        copy = pltpu.make_async_copy(res.at[groups], res_hbm.at[groups], store_sem.at[at])
        copy.start()
        return copy

    finals = []
    for _ in range(3):
        for part, (base, n, _) in zip(state, PARTS):
            if part["wait"] is None:
                continue
            for copy in part["wait"]:
                copy.wait_recv()
            if part["path"]:
                gather(part)
            else:
                part["wait"] = None
                region = res.at[pl.ds(mine + base, n)]
                finals.append((start(region, region, twin), base, n))
    stores = []
    for _, base, n in finals:
        stores.append(store(len(stores), mine, base, n))
    for copy, base, n in finals:
        copy.wait_recv()
        stores.append(store(len(stores), theirs, base, n))

    for copy in [keep_u, keep_handed, *stores]:
        copy.wait()
    for copy in started:
        copy.wait_send()
    for p in range(len(PIECES)):
        for copy in piece_copies(p):
            copy.wait_send()
        if p < RELAYED:
            crossing(p).wait_send()

    @pl.when(d < depths - 1)
    def _():
        for at in range(count + PANELS - 1):
            handed_copy(at).wait_send()


def tile_of(i, j):
    delta = (j - i) % MB
    if delta > MB // 2 or (delta == MB // 2 and i >= MB // 2):
        return tile_of(j, i)[0], True
    if delta == MB // 2:
        return (i // 2) * HALF_TILES + 16 + i % 2, False
    return (i // 4) * HALF_TILES + delta * 4 + i % 4, False


def finish_kernel(
    u_hbm, handed_hbm, res_hbm, tip_hbm, lower_hbm, given_hbm, out_hbm,
    u, handed, res, tip, lower, out, sems, row_sems, out_sems,
):
    load_u = pltpu.make_async_copy(u_hbm, u, sems.at[0])
    load_handed = pltpu.make_async_copy(handed_hbm, handed, sems.at[1])
    load_res = [
        pltpu.make_async_copy(res_hbm.at[pl.ds(h * HALF, HALF)], res.at[pl.ds(h * HALF, HALF)], sems.at[2 + h])
        for h in range(2)
    ]
    kept = pltpu.make_async_copy(lower, lower_hbm, sems.at[4])
    given = pltpu.make_async_copy(handed, given_hbm, sems.at[5])
    row_loads, row_stores = [], []
    for i in range(MB):
        rows = pl.ds(i * BS, BS)
        row_loads.append(pltpu.make_async_copy(tip_hbm.at[rows], tip.at[rows], row_sems.at[i]))
        row_stores.append(pltpu.make_async_copy(out.at[rows], out_hbm.at[rows], out_sems.at[i]))
    for copy in [load_u, load_handed, *load_res, *row_loads]:
        copy.start()
    row = lax.broadcasted_iota(jnp.int32, (BS, BS), 0)
    col = lax.broadcasted_iota(jnp.int32, (BS, BS), 1)
    load_u.wait()
    for n in range(u.shape[0]):
        un = u[n]
        lower[n] = jnp.where(col > row, un, jnp.where(col == row, 1.0 / un, 0.0)).T
    kept.start()
    load_handed.wait()
    given.start()
    for copy in load_res:
        copy.wait()
    for i in range(MB):
        row_loads[i].wait()
        for j in range(MB):
            at, turned = tile_of(i, j)
            value = res[at * 16 : at * 16 + 16].reshape(BS, BS)
            here = (slice(i * BS, i * BS + BS), slice(j * BS, j * BS + BS))
            out[here] = tip[here] - (value.T if turned else value)
        row_stores[i].start()
    for copy in [given, kept, *row_stores]:
        copy.wait()


def body(diag_blocks, coupling, offsets, arrow_blocks, arrow_index, tip):
    count, width = offsets.shape[1:]
    spokes = arrow_index.shape[2]
    copies, room = 2 * len(PARTS) + SIZES["y"] - 1, 0
    for _, n, order in PARTS:
        for axis in order:
            n //= SIZES[axis]
            room += (SIZES[axis] - 1) * n
            copies += 2 * (SIZES[axis] - 1)
    smem, hbm = (pl.BlockSpec(memory_space=space) for space in (pltpu.SMEM, pl.ANY))
    blocks = jax.ShapeDtypeStruct((count, BS, BS), F32)
    band = 2 * REACH + count
    dma = pltpu.SemaphoreType.DMA
    u, handed, total = pl.pallas_call(
        kernel,
        out_shape=(blocks, blocks, jax.ShapeDtypeStruct((2 * HALF, 8, BS), F32)),
        in_specs=[hbm, hbm, smem, hbm, smem],
        out_specs=(hbm, hbm, hbm),
        scratch_shapes=[
            pltpu.VMEM((count, BS, BS), F32),
            pltpu.VMEM((count, BS, BS), F32),
            pltpu.VMEM((count, BS, BS), F32),
            pltpu.VMEM((count * width, BS, BS), F32),
            pltpu.VMEM((count, spokes, BS, BS), F32),
            pltpu.VMEM((count, BS, BS), F32),
            pltpu.VMEM((count, BS, BS), F32),
            tuple(pltpu.VMEM((5 * blocks, last - first, BS), F32) for _, _, blocks, first, last in PIECES),
            pltpu.VMEM((band, BS, 2 * BS), BF16),
            pltpu.VMEM((count * width, 2 * BS, 2 * BS), BF16),
            pltpu.VMEM((count, 3 * BS, spokes * BS), BF16),
            pltpu.VMEM((count, width * BS, 2 * BS), BF16),
            pltpu.VMEM((count, spokes + 1, 2, BS, BS), BF16),
            pltpu.VMEM((count * BS, 12 * BS), BF16),
            pltpu.VMEM((count * BS, 12 * BS), BF16),
            pltpu.VMEM((2 * HALF, 8, BS), F32),
            pltpu.VMEM((HALF, 8, BS), F32),
            pltpu.VMEM((HALF, 8, BS), F32),
            pltpu.VMEM((room, 8, BS), F32),
            pltpu.VMEM((SIZES["y"], 1, 8, BS), F32),
            pltpu.VMEM((2 * HALF, 8, BS), F32),
            dma((3,)),
            dma((2 * len(PARTS),)),
            dma((2,)),
            dma((len(PIECES), 4)),
            dma((len(PIECES), 4)),
            dma((count + PANELS - 1,)),
            dma((count + PANELS - 1,)),
            dma((copies,)),
            dma((copies,)),
        ],
        compiler_params=pltpu.CompilerParams(
            collective_id=0, has_side_effects=True, vmem_limit_bytes=60 * 1024 * 1024
        ),
    )(diag_blocks[0], coupling[0].reshape(count * width, BS, BS), offsets[0], arrow_blocks[0], arrow_index[0])
    lower, handed, schur_tip = pl.pallas_call(
        finish_kernel,
        out_shape=(blocks, blocks, jax.ShapeDtypeStruct(tip.shape, F32)),
        in_specs=[hbm] * 4,
        out_specs=(hbm,) * 3,
        scratch_shapes=[
            pltpu.VMEM(blocks.shape, F32),
            pltpu.VMEM(blocks.shape, F32),
            pltpu.VMEM(total.shape, F32),
            pltpu.VMEM(tip.shape, F32),
            pltpu.VMEM(blocks.shape, F32),
            pltpu.VMEM(tip.shape, F32),
            dma((6,)),
            dma((MB,)),
            dma((MB,)),
        ],
        compiler_params=pltpu.CompilerParams(vmem_limit_bytes=60 * 1024 * 1024),
    )(u, handed, total, tip)
    return (lower[None], handed[None], schur_tip)


def solution(mesh):
    return jax.shard_map(
        body,
        mesh=mesh,
        in_specs=(
            P("depth", "lat", None, None),
            P("depth", "lat", None, None, None),
            P("depth", "lat", None),
            P("depth", "lat", None, None, None),
            P("depth", "lat", None),
            P(),
        ),
        out_specs=(P("depth", "lat", None, None), P("depth", "lat", None, None), P()),
        check_vma=False,
    )
```

```python
import functools

import jax
import jax.numpy as jnp
from jax import lax
from jax.experimental import pallas as pl
from jax.experimental.pallas import tpu as pltpu
from jax.sharding import PartitionSpec as P

BS = 128
PANEL = 32
PANELS = BS // PANEL
REACH = 8
MB = 8
F32 = jnp.float32
BF16 = jnp.bfloat16
MESH = pl.DeviceIdType.MESH
X, Z = 4, 8
SIZES = {"x": X, "y": 4, "z": Z}
HALF_TILES = 18
HALF = HALF_TILES * 16
PARTS = ((0, 128, "xyz"), (128, 128, "yxz"), (256, 32, "zx"))
PIECES = (
    (64, "pair", 2, 0, 32), (80, "top", 4, 0, 16), (96, "top", 4, 16, 32), (112, "all", 4, 0, 16), (128, "all", 4, 16, 32)
)
RELAYED = 4
EARLY = 3


def split2(x):
    high = x.astype(BF16)
    return high, (x - high.astype(F32)).astype(BF16)


def split3(x):
    high = x.astype(BF16)
    rest = x - high.astype(F32)
    middle = rest.astype(BF16)
    return high, middle, (rest - middle.astype(F32)).astype(BF16)


def dot(a, b):
    return jnp.dot(a, b, preferred_element_type=F32)


def dot_t(a, b):
    return lax.dot_general(a, b, (((0,), (0,)), ((), ())), preferred_element_type=F32)


def gram_exact(u, v):
    uh, um, ul = split3(u)
    vh, vm, vl = split3(v)
    return dot_t(
        jnp.concatenate([uh, uh, uh, um, um, ul], 0),
        jnp.concatenate([vh, vm, vl, vh, vm, vh], 0),
    )


def eliminate(part, j0, done):
    count = part[0].shape[0]
    shape = (count, 8, BS)
    lane = lax.broadcasted_iota(jnp.int32, shape, 2)
    sub = lax.broadcasted_iota(jnp.int32, shape, 1)
    groups = len(part)
    spread = lambda x: jnp.broadcast_to(x, shape)
    for g in range(groups):
        c0 = j0 + 8 * g
        cols = [[spread(part[v][:, :, c0 + k : c0 + k + 1]) for k in range(8)] for v in range(g, groups)]
        keep = (lane < c0) | (lane >= c0 + 8)
        x = jnp.where(keep, part[g], jnp.where(lane == c0 + sub, 1.0, 0.0))
        d = cols[0]
        scales, rows, low = [], [], {}
        for i in range(8):
            scale = lax.rsqrt(spread(d[i][:, i : i + 1, :]))
            li = d[i] * scale
            for k in range(i + 1, 8):
                low[k, i] = spread(li[:, k : k + 1, :])
                d[k] = d[k] - li * low[k, i]
            row = spread(x[:, i : i + 1, :]) * scale
            scales.append(scale)
            rows.append(row)
            x = jnp.where(sub > i, x - li * row, jnp.where(sub == i, row, x))
        for k in range(1, 8):
            for i in range(k):
                x = jnp.where((sub == i) & (lane == c0 + k), low[k, i], x)
        part[g] = x
        for v in range(g + 1, groups):
            d = cols[v - g]
            x = jnp.where(keep, part[v], 0.0)
            for i in range(8):
                mi = d[i] * scales[i]
                for k in range(i + 1, 8):
                    d[k] = d[k] - mi * low[k, i]
                x = x - mi * rows[i]
            part[v] = x
        done(g)


def kernel(
    diag_hbm, coup_hbm, off_ref, arrow_hbm, idx_ref,
    u_hbm, handed_hbm, res_hbm,
    ubuf, handed_ref, dbuf, cbuf, bbuf, corr, landed, pieces, wide, cwide, bwide, stacked, placed, hi, lo,
    g_ref, other, acc, bufs, ring, res,
    load_sem, store_sem, keep_sem, win_send, win_recv, dep_send, dep_recv, sum_send, sum_recv,
):
    depths, lats = lax.axis_size("depth"), lax.axis_size("lat")
    d, l = lax.axis_index("depth"), lax.axis_index("lat")
    count, width = off_ref.shape
    spokes = idx_ref.shape[1]
    px, pz, c = l // (2 * Z), lax.rem(l // 2, Z), lax.rem(l, 2)
    place = {"x": px, "y": d, "z": pz}
    twin = (d, l + 1 - 2 * c)

    def device(axis, index):
        if axis == "y":
            return (index, l)
        if axis == "x":
            return (d, (index * Z + pz) * 2 + c)
        return (d, (px * Z + index) * 2 + c)

    def lat_at(step):
        return (d, lax.rem(l + step + lats, lats))

    def remote(src, dst, send, recv, peer):
        return pltpu.make_async_remote_copy(
            src_ref=src, dst_ref=dst, send_sem=send, recv_sem=recv, device_id=peer, device_id_type=MESH
        )

    loads = [
        pltpu.make_async_copy(src, dst, load_sem.at[at])
        for at, (src, dst) in enumerate(((diag_hbm, dbuf), (coup_hbm, cbuf), (arrow_hbm, bbuf)))
    ]
    loads[0].start()

    keep_u = pltpu.make_async_copy(ubuf, u_hbm, keep_sem.at[0])
    keep_handed = pltpu.make_async_copy(handed_ref, handed_hbm, keep_sem.at[1])

    barrier = pltpu.get_barrier_semaphore()
    peers = [twin, lat_at(-2), lat_at(2), lat_at(2 * c - 1)]
    for axis in "xyz":
        peers += [device(axis, lax.rem(place[axis] + off, SIZES[axis])) for off in range(1, SIZES[axis])]
    for peer in peers:
        pl.semaphore_signal(barrier, inc=1, device_id=peer, device_id_type=MESH)

    def split_coupling():
        def couple(at, _):
            ch, cl = split2(cbuf[at])
            cwide[at] = jnp.concatenate(
                [jnp.concatenate([ch, cl], 1), jnp.concatenate([ch, jnp.zeros_like(ch)], 1)], 0
            )
            return 0

        loads[1].wait()
        lax.fori_loop(0, count * width, couple, 0)

    def split_spokes():
        def spoke(n, _):
            for s in range(spokes):
                bh, bl = split2(bbuf[n, s])
                bwide[n, :, s * BS : (s + 1) * BS] = jnp.concatenate([bh, bh, bl], 0)
            placed[n, spokes] = jnp.zeros(placed.shape[2:], BF16)
            return 0

        loads[2].wait()
        lax.fori_loop(0, count, spoke, 0)

    def handed_copy(at):
        if at < count:
            rows = (at, pl.ds(0, PANEL))
        else:
            rows = (slice(None), pl.ds((at - count + 1) * PANEL, PANEL))
        return remote(
            handed_ref.at[rows], landed.at[rows], dep_send.at[at], dep_recv.at[at],
            (lax.rem(d + 1, depths), l),
        )

    @pl.when(d == 0)
    def _():
        landed[...] = jnp.zeros_like(landed)

    loads[0].wait()
    loads[1].start()
    loads[2].start()

    @pl.when(d > 0)
    def _():
        split_coupling()
        split_spokes()

    def place_of(step, p):
        blocks = PIECES[p][2]
        return pieces[p].at[pl.ds(step * blocks, blocks)]

    def received(p, at, step):
        return remote(place_of(2, p), place_of(step, p), win_send.at[p, at], win_recv.at[p, at], twin)

    def piece_copies(p):
        own = place_of(2, p)
        copies = [
            remote(own, place_of(4, p), win_send.at[p, 0], win_recv.at[p, 0], lat_at(-2)),
            remote(own, place_of(0, p), win_send.at[p, 1], win_recv.at[p, 1], lat_at(2)),
            remote(own, place_of(1 + 2 * c, p), win_send.at[p, 2], win_recv.at[p, 2], twin),
        ]
        if p >= RELAYED:
            copies.append(crossing(p))
        return copies

    def crossing(p):
        if p < RELAYED:
            src, peer = place_of(4 - 4 * c, p), twin
        else:
            src, peer = place_of(2, p), lat_at(2 * c - 1)
        return remote(src, place_of(3 - 2 * c, p), win_send.at[p, 3], win_recv.at[p, 3], peer)

    def hand_over(p):
        received(p, c, 4 - 4 * c).wait_recv()
        if p < RELAYED:
            crossing(p).start()

    def wait_piece(p):
        received(p, 1 - c, 4 * c).wait_recv()
        received(p, 2, 1 + 2 * c).wait_recv()
        crossing(p).wait_recv()

    def pack(p):
        end, kind, blocks, first, last = PIECES[p]
        rows = end - (last - first)
        value = ubuf[:, rows:end, :]
        lane = lax.broadcasted_iota(jnp.int32, value.shape, 2)
        value = jnp.where(lane <= rows + lax.broadcasted_iota(jnp.int32, value.shape, 1), value, 0.0)
        if kind == "pair":
            half = lane[:2] < BS // 2
            value = jnp.where(half, value[:2], pltpu.roll(value[2:], BS // 2, 2))
        elif kind == "top":
            top = ubuf[:, first:last, :]
            top = jnp.where(lane <= first + lax.broadcasted_iota(jnp.int32, top.shape, 1), top, 0.0)
            value = jnp.where(lane < BS - PANEL, value, pltpu.roll(top, BS - PANEL, 2))
        pieces[p][2 * blocks : 3 * blocks] = value

    def widen(rows, blocks, value):
        high, low = split2(value)
        wide[blocks, rows, :] = jnp.concatenate([high, low], 2)

    def unpack(which):
        for step in range(5):
            inside = (l + step >= 2) & (l + step < lats + 2)
            at = step * count
            for p in which:
                end, kind, blocks, first, last = PIECES[p]
                rows = slice(end - (last - first), end)
                value = jnp.where(inside, pieces[p][step * blocks : (step + 1) * blocks], 0.0)
                lane = lax.broadcasted_iota(jnp.int32, value.shape, 2)
                if kind == "pair":
                    half = lane < BS // 2
                    widen(rows, slice(at, at + 2), jnp.where(half, value, 0.0))
                    widen(rows, slice(at + 2, at + 4), jnp.where(half, pltpu.roll(value, BS // 2, 2), 0.0))
                elif kind == "top":
                    widen(rows, slice(at, at + count), jnp.where(lane < BS - PANEL, value, 0.0))
                    top = jnp.where(lane < PANEL, pltpu.roll(value, PANEL, 2), 0.0)
                    widen(slice(first, last), slice(at, at + count), top)
                else:
                    widen(rows, slice(at, at + count), value)

    for p in range(PANELS):
        j0, end = p * PANEL, (p + 1) * PANEL
        needed = (count + p - 1,) if p else range(count)

        @pl.when(d > 0)
        def _():
            for at in needed:
                handed_copy(at).wait_recv()

        a = dbuf[:, j0:end, :] + landed[:, j0:end, :]
        lane = lax.broadcasted_iota(jnp.int32, a.shape, 2)
        row = j0 + lax.broadcasted_iota(jnp.int32, a.shape, 1)
        if p:
            a = jnp.where(lane < j0, 0.0, a) - corr[:, j0:end, :]
        part = [a[:, 8 * v : 8 * v + 8] for v in range(PANEL // 8)]

        def done(g):
            if g % 2 == 0:
                return
            row = j0 + 8 * g - 8
            ubuf[:, row : row + 16, :] = jnp.concatenate(part[g - 1 : g + 1], 1)
            for at, piece in enumerate(PIECES):
                if piece[0] == row + 16:
                    pack(at)
                    if at == 0:
                        pl.semaphore_wait(barrier, len(peers))
                    for copy in piece_copies(at):
                        copy.start()
            if row + 16 == 112:
                hand_over(0)

        eliminate(part, j0, done)
        if end < BS:
            u = jnp.concatenate(part, 1)
            right = jnp.where((lane < end) & (lane > row), 0.0, u)
            for m in range(count):
                full = gram_exact(u[m], right[m])[end:]
                if p:
                    old = corr[m, end:, :]
                    ln = lax.broadcasted_iota(jnp.int32, old.shape, 1)
                    full = full + jnp.where((ln >= j0) & (ln < end), 0.0, old)
                corr[m, end:, :] = full

    def update(hand_on):
        for p in range(1, EARLY):
            hand_over(p)

        @pl.when(d == 0)
        def _():
            split_coupling()

        for p in range(EARLY, RELAYED):
            hand_over(p)
        for p in range(EARLY):
            wait_piece(p)
        unpack(range(EARLY))
        for p in range(RELAYED, len(PIECES)):
            hand_over(p)
        for p in range(EARLY, len(PIECES)):
            wait_piece(p)
        unpack(range(EARLY, len(PIECES)))
        for m in range(count):
            for w in range(width):
                x = dot(wide[off_ref[m, w] + (m + REACH)], cwide[m * width + w])
                xh, xl = split2(x[:, :BS] + x[:, BS:])
                stacked[m, w * BS : (w + 1) * BS, :] = jnp.concatenate([xh, xl], 1)
        for m in range(count):
            both = dot_t(stacked[m, :, :BS], stacked[m])
            cross = both[:, BS:]
            handed_ref[m] = -(both[:, :BS] + cross + cross.T)
            if hand_on:
                handed_copy(m).start()
        if hand_on:
            for p in range(1, PANELS):
                handed_copy(count + p - 1).start()
        keep_handed.start()

    keep_u.start()

    @pl.when(d < depths - 1)
    def _():
        update(True)

    @pl.when(d == 0)
    def _():
        split_spokes()

    row = lax.broadcasted_iota(jnp.int32, (BS, BS), 0)
    col = lax.broadcasted_iota(jnp.int32, (BS, BS), 1)
    for n in range(count):
        high, low = split2(jnp.where(col <= row, ubuf[n], 0.0))
        t = dot(jnp.concatenate([high, low, high], 1), bwide[n])
        for s in range(spokes):
            th, tl = split2(t[:, s * BS : (s + 1) * BS])
            placed[n, s, 0] = th
            placed[n, s, 1] = tl
    for n in range(count):
        for m in range(MB):
            slot = spokes
            for s in range(spokes):
                slot = jnp.where(idx_ref[n, s] == m, s, slot)
            both = placed[n, slot]
            for at in (m, m + MB)[: 2 if m < MB // 2 else 1]:
                hi[n * BS : (n + 1) * BS, at * BS : (at + 1) * BS] = both[0]
                lo[n * BS : (n + 1) * BS, at * BS : (at + 1) * BS] = both[1]

    def tile_product(i, first, tiles):
        left = pl.ds(pl.multiple_of(i * BS, BS), BS)
        right = pl.ds(pl.multiple_of(first * BS, BS), tiles * BS)
        high, n = hi[:, right], tiles * BS
        both = dot_t(hi[:, left], jnp.concatenate([high, lo[:, right]], 1))
        return both[:, :n] + both[:, n:] + dot_t(lo[:, left], high)

    def put(h, k, value):
        g_ref[pl.ds((h * HALF_TILES + k) * 16, 16)] = value.reshape(16, 8, BS)

    def half_products(h):
        for ii in range(4):
            product = tile_product(4 * h + ii, 4 * h + ii, 4)
            for delta in range(4):
                put(h, delta * 4 + ii, product[:, delta * BS : (delta + 1) * BS])
        for ii in range(2):
            put(h, 16 + ii, tile_product(2 * h + ii, 2 * h + ii + 4, 1))

    used = [0]
    started = []

    def start(src, dst, peer):
        at = used[0]
        used[0] += 1
        copy = remote(src, dst, sum_send.at[at], sum_recv.at[at], peer)
        copy.start()
        started.append(copy)
        return copy

    mine, theirs = c * HALF, (1 - c) * HALF
    half_products(1 - c)
    arriving = [start(g_ref.at[pl.ds(theirs + at, n)], other.at[pl.ds(at, n)], twin) for at, n, _ in PARTS]
    half_products(c)
    slot = [0]

    def scatter(part):
        axis = part["order"][part["phase"]]
        k, here = SIZES[axis], place[axis]
        base, piece = part["base"], part["n"] // k
        part["wait"] = []
        for off in range(1, k):
            to = lax.rem(here + off, k)
            copy = start(
                acc.at[pl.ds(base + to * piece, piece)], bufs.at[pl.ds(slot[0], piece)], device(axis, to)
            )
            part["wait"].append((copy, slot[0]))
            slot[0] += piece
        part["base"], part["n"], part["phase"] = base + here * piece, piece, part["phase"] + 1
        part["path"].append((axis, part["base"], piece))

    def collect(part):
        own = pl.ds(part["base"], part["n"])
        value = acc[own]
        for copy, at in part["wait"]:
            copy.wait_recv()
            value = value + bufs[at : at + part["n"]]
        acc[own] = value

    state = []
    for copy, (base, n, order) in zip(arriving, PARTS):
        copy.wait_recv()
        acc[base : base + n] = g_ref[pl.ds(mine + base, n)] + other[base : base + n]
        part = {"base": base, "n": n, "order": order, "phase": 0, "path": []}
        state.append(part)
        scatter(part)

    @pl.when(d == depths - 1)
    def _():
        update(False)

    for phase in range(3):
        for part in state:
            if phase < len(part["order"]):
                collect(part)
                if phase + 1 < len(part["order"]):
                    scatter(part)
    last = state[-1]
    own = pl.ds(last["base"], last["n"])
    ring[d] = acc[own]
    copies = []
    for off in range(1, SIZES["y"]):
        to = lax.rem(d + off, SIZES["y"])
        copies.append(start(acc.at[own], ring.at[d], device("y", to)))
    for part in state[:-1]:
        res[pl.ds(mine + part["base"], part["n"])] = acc[pl.ds(part["base"], part["n"])]

    def gather(part):
        axis, base, n = part["path"].pop()
        k, here = SIZES[axis], place[axis]
        region = res.at[pl.ds(mine + base, n)]
        part["wait"] = [start(region, region, device(axis, lax.rem(here + off, k))) for off in range(1, k)]

    for part in state[:-1]:
        gather(part)
    for copy in copies:
        copy.wait_recv()
    value = ring[0]
    for at in range(1, SIZES["y"]):
        value = value + ring[at]
    res[pl.ds(mine + last["base"], last["n"])] = value
    gather(last)

    def store(at, half, base, n):
        groups = pl.ds(half + base, n)
        copy = pltpu.make_async_copy(res.at[groups], res_hbm.at[groups], store_sem.at[at])
        copy.start()
        return copy

    finals = []
    for _ in range(3):
        for part, (base, n, _) in zip(state, PARTS):
            if part["wait"] is None:
                continue
            for copy in part["wait"]:
                copy.wait_recv()
            if part["path"]:
                gather(part)
            else:
                part["wait"] = None
                region = res.at[pl.ds(mine + base, n)]
                finals.append((start(region, region, twin), base, n))
    stores = []
    for _, base, n in finals:
        stores.append(store(len(stores), mine, base, n))
    for copy, base, n in finals:
        copy.wait_recv()
        stores.append(store(len(stores), theirs, base, n))

    for copy in [keep_u, keep_handed, *stores]:
        copy.wait()
    for copy in started:
        copy.wait_send()
    for p in range(len(PIECES)):
        for copy in piece_copies(p):
            copy.wait_send()
        if p < RELAYED:
            crossing(p).wait_send()

    @pl.when(d < depths - 1)
    def _():
        for at in range(count + PANELS - 1):
            handed_copy(at).wait_send()


def tile_of(i, j):
    delta = (j - i) % MB
    if delta > MB // 2 or (delta == MB // 2 and i >= MB // 2):
        return tile_of(j, i)[0], True
    if delta == MB // 2:
        return (i // 2) * HALF_TILES + 16 + i % 2, False
    return (i // 4) * HALF_TILES + delta * 4 + i % 4, False


def finish_kernel(
    u_hbm, handed_hbm, res_hbm, tip_hbm, lower_hbm, given_hbm, out_hbm,
    u, handed, res, tip, lower, out, sems, row_sems, out_sems,
):
    load_u = pltpu.make_async_copy(u_hbm, u, sems.at[0])
    load_handed = pltpu.make_async_copy(handed_hbm, handed, sems.at[1])
    load_res = [
        pltpu.make_async_copy(res_hbm.at[pl.ds(h * HALF, HALF)], res.at[pl.ds(h * HALF, HALF)], sems.at[2 + h])
        for h in range(2)
    ]
    kept = pltpu.make_async_copy(lower, lower_hbm, sems.at[4])
    given = pltpu.make_async_copy(handed, given_hbm, sems.at[5])
    row_loads, row_stores = [], []
    for i in range(MB):
        rows = pl.ds(i * BS, BS)
        row_loads.append(pltpu.make_async_copy(tip_hbm.at[rows], tip.at[rows], row_sems.at[i]))
        row_stores.append(pltpu.make_async_copy(out.at[rows], out_hbm.at[rows], out_sems.at[i]))
    for copy in [load_u, load_handed, *load_res, *row_loads]:
        copy.start()
    row = lax.broadcasted_iota(jnp.int32, (BS, BS), 0)
    col = lax.broadcasted_iota(jnp.int32, (BS, BS), 1)
    load_u.wait()
    for n in range(u.shape[0]):
        un = u[n]
        lower[n] = jnp.where(col > row, un, jnp.where(col == row, 1.0 / un, 0.0)).T
    kept.start()
    load_handed.wait()
    given.start()
    for copy in load_res:
        copy.wait()
    for i in range(MB):
        row_loads[i].wait()
        for j in range(MB):
            at, turned = tile_of(i, j)
            value = res[at * 16 : at * 16 + 16].reshape(BS, BS)
            here = (slice(i * BS, i * BS + BS), slice(j * BS, j * BS + BS))
            out[here] = tip[here] - (value.T if turned else value)
        row_stores[i].start()
    for copy in [given, kept, *row_stores]:
        copy.wait()


def body(diag_blocks, coupling, offsets, arrow_blocks, arrow_index, tip):
    count, width = offsets.shape[1:]
    spokes = arrow_index.shape[2]
    copies, room = 2 * len(PARTS) + SIZES["y"] - 1, 0
    for _, n, order in PARTS:
        for axis in order:
            n //= SIZES[axis]
            room += (SIZES[axis] - 1) * n
            copies += 2 * (SIZES[axis] - 1)
    smem, hbm = (pl.BlockSpec(memory_space=space) for space in (pltpu.SMEM, pl.ANY))
    blocks = jax.ShapeDtypeStruct((count, BS, BS), F32)
    band = 2 * REACH + count
    dma = pltpu.SemaphoreType.DMA
    u, handed, total = pl.pallas_call(
        kernel,
        out_shape=(blocks, blocks, jax.ShapeDtypeStruct((2 * HALF, 8, BS), F32)),
        in_specs=[hbm, hbm, smem, hbm, smem],
        out_specs=(hbm, hbm, hbm),
        scratch_shapes=[
            pltpu.VMEM((count, BS, BS), F32),
            pltpu.VMEM((count, BS, BS), F32),
            pltpu.VMEM((count, BS, BS), F32),
            pltpu.VMEM((count * width, BS, BS), F32),
            pltpu.VMEM((count, spokes, BS, BS), F32),
            pltpu.VMEM((count, BS, BS), F32),
            pltpu.VMEM((count, BS, BS), F32),
            tuple(pltpu.VMEM((5 * blocks, last - first, BS), F32) for _, _, blocks, first, last in PIECES),
            pltpu.VMEM((band, BS, 2 * BS), BF16),
            pltpu.VMEM((count * width, 2 * BS, 2 * BS), BF16),
            pltpu.VMEM((count, 3 * BS, spokes * BS), BF16),
            pltpu.VMEM((count, width * BS, 2 * BS), BF16),
            pltpu.VMEM((count, spokes + 1, 2, BS, BS), BF16),
            pltpu.VMEM((count * BS, 12 * BS), BF16),
            pltpu.VMEM((count * BS, 12 * BS), BF16),
            pltpu.VMEM((2 * HALF, 8, BS), F32),
            pltpu.VMEM((HALF, 8, BS), F32),
            pltpu.VMEM((HALF, 8, BS), F32),
            pltpu.VMEM((room, 8, BS), F32),
            pltpu.VMEM((SIZES["y"], 1, 8, BS), F32),
            pltpu.VMEM((2 * HALF, 8, BS), F32),
            dma((3,)),
            dma((2 * len(PARTS),)),
            dma((2,)),
            dma((len(PIECES), 4)),
            dma((len(PIECES), 4)),
            dma((count + PANELS - 1,)),
            dma((count + PANELS - 1,)),
            dma((copies,)),
            dma((copies,)),
        ],
        compiler_params=pltpu.CompilerParams(
            collective_id=0, has_side_effects=True, vmem_limit_bytes=60 * 1024 * 1024
        ),
    )(diag_blocks[0], coupling[0].reshape(count * width, BS, BS), offsets[0], arrow_blocks[0], arrow_index[0])
    lower, handed, schur_tip = pl.pallas_call(
        finish_kernel,
        out_shape=(blocks, blocks, jax.ShapeDtypeStruct(tip.shape, F32)),
        in_specs=[hbm] * 4,
        out_specs=(hbm,) * 3,
        scratch_shapes=[
            pltpu.VMEM(blocks.shape, F32),
            pltpu.VMEM(blocks.shape, F32),
            pltpu.VMEM(total.shape, F32),
            pltpu.VMEM(tip.shape, F32),
            pltpu.VMEM(blocks.shape, F32),
            pltpu.VMEM(tip.shape, F32),
            dma((6,)),
            dma((MB,)),
            dma((MB,)),
        ],
        compiler_params=pltpu.CompilerParams(vmem_limit_bytes=60 * 1024 * 1024),
    )(u, handed, total, tip)
    return (lower[None], handed[None], schur_tip)


def solution(mesh):
    return jax.shard_map(
        body,
        mesh=mesh,
        in_specs=(
            P("depth", "lat", None, None),
            P("depth", "lat", None, None, None),
            P("depth", "lat", None),
            P("depth", "lat", None, None, None),
            P("depth", "lat", None),
            P(),
        ),
        out_specs=(P("depth", "lat", None, None), P("depth", "lat", None, None), P()),
        check_vma=False,
    )
```
